32 devices in a mesh: img: 16 (over z, y, core), ori: 2 (over x).
Axes of the slice: x: 2, y: 2, z: 4, core: 2. Of those that a mesh axis runs over, the one named last changes fastest.
Arguments:
- images: float32 [4096, 2048], P(('img', 'ori')), may hold values from -40 to 40
- precision: float32 [4096], P('img'), may hold values from 0.5 to 2
- projections: bfloat16 [8192, 2048], P('ori'), may hold values from -1 to 1
- tile_mask: int32 [32, 64], P('img', 'ori'), may hold values from 0 to 1, as said below
Outputs:
- posteriors: bfloat16 [4096, 8192], P('img', 'ori')
- references: float32 [8192, 2048], P(('ori', 'img'))
The draws below stay inside these ranges and needn't reach their ends.
Inputs may be any that keep to these rules, and one draw needn't show every extreme that they name: `tile_mask`: every image block has at least one live tile.
All inputs are finite; a program needn't handle non-finite values.
Results may differ from the reference program's by a relative error of at most 0.0095.
Values may be sent and summed in bfloat16 or wider, within the bound.
No kernel may reach another device: no remote copies, remote signals or barrier semaphores. Data moves between devices by JAX's collectives and lax.ppermute only.
A program may use at most 128 MiB of HBM per device.

```python
import math
import jax
import jax.numpy as jnp
from jax import lax

K = 2048
ORIENT = 8192
TILE = 128
IMG_DEV = 128
IMAGES = 4096
BLOCKS = 32
TILES = 64
N_IMG = 16
N_ORI = 2


def unit_table(key):
    table = jax.random.normal(jax.random.fold_in(key, 101), (ORIENT, K), jnp.float32)
    return table / jnp.sqrt(jnp.sum(table * table, axis=1, keepdims=True))


def draw_projections(key, part):
    table = unit_table(key)
    return table.astype(jnp.bfloat16)


def draw_images(key, part):
    noise_key = jax.random.fold_in(key, 102)
    result = jax.random.normal(noise_key, (IMAGES, K), jnp.float32)
    return jnp.clip(result, -40.0, 40.0)


def draw_tile_mask(key, part):
    spread = jax.random.randint(jax.random.fold_in(key, 201), (BLOCKS, 1), 100, 1000)
    cutoff = spread * spread // 1000
    levels = jax.random.randint(jax.random.fold_in(key, 202), (BLOCKS, TILES), 0, 1000)
    forced = jax.random.randint(jax.random.fold_in(key, 203), (BLOCKS, 1), 0, TILES)
    columns = jnp.arange(TILES, dtype=jnp.int32)[None, :]
    return jnp.where((levels < cutoff) | (columns == forced), 1, 0).astype(jnp.int32)


def block_levels(stream_key, dims, shards, smallest, largest):
    level = 1.0
    for dim, parts in shards:
        steps = jax.random.uniform(jax.random.fold_in(jax.random.fold_in(stream_key, 6), dim), (parts,), jnp.float32, smallest / len(shards), largest / len(shards))
        level = level * jnp.repeat(jnp.exp(steps), dims[dim] // parts).reshape((-1,) + (1,) * (len(dims) - 1 - dim))
    return level


def setup_inputs(seed: int = 0) -> dict:
    arg_keys = jax.random.split(jax.random.key(seed), 5)
    return {
        "images": draw_images(jax.random.fold_in(arg_keys[4], 71), 0),
        "precision": jnp.clip(jnp.exp(math.log(2.0) - 1.3862944 * jax.random.uniform(arg_keys[1], (IMAGES,), jnp.float32) ** block_levels(arg_keys[1], (IMAGES,), ((0, 16),), -0.2, 0.2)), 0.5, 2.0),
        "projections": draw_projections(jax.random.fold_in(arg_keys[4], 71), 0),
        "tile_mask": draw_tile_mask(jax.random.fold_in(arg_keys[4], 71), 0),
    }


prior_weight = 1.0


def reference(images, precision, projections, tile_mask):
    group_rows = IMG_DEV * N_ORI
    proj_float = projections.astype(jnp.float32)
    squared = jnp.sum(proj_float * proj_float, axis=1)

    def one_group(running, group_index):
        sums_now, counts_now = running
        first_row = (group_index * group_rows).astype(jnp.int32)
        lowered = lax.dynamic_slice_in_dim(images, first_row, group_rows, 0).astype(jnp.bfloat16)
        weights_here = lax.dynamic_slice_in_dim(precision, first_row, group_rows, 0)
        mask_rows = lax.dynamic_slice_in_dim(tile_mask, (group_index * N_ORI).astype(jnp.int32), N_ORI, 0)
        alive = jnp.repeat(jnp.repeat(mask_rows > 0, IMG_DEV, axis=0), TILE, axis=1)
        products = lax.dot_general(lowered, projections, (((1,), (1,)), ((), ())), preferred_element_type=jnp.float32)
        scores = weights_here[:, None] * (products - 0.5 * squared[None, :])
        highest = jnp.max(jnp.where(alive, scores, -jnp.inf), axis=1, keepdims=True)
        lifted = jnp.where(alive, jnp.exp(jnp.where(alive, scores - highest, -jnp.inf)), 0.0)
        posterior = (lifted / jnp.sum(lifted, axis=1, keepdims=True)).astype(jnp.bfloat16)
        sums_now = sums_now + lax.dot_general(posterior, lowered, (((0,), (0,)), ((), ())), preferred_element_type=jnp.float32)
        counts_now = counts_now + jnp.sum(posterior.astype(jnp.float32), axis=0)
        return (sums_now, counts_now), posterior

    start_state = (jnp.zeros((ORIENT, K), jnp.float32), jnp.zeros((ORIENT,), jnp.float32))
    (summed, counts), posts = lax.scan(one_group, start_state, jnp.arange(N_IMG, dtype=jnp.int32))
    posteriors = posts.reshape(IMAGES, ORIENT)
    references = (summed + prior_weight * proj_float) / (counts[:, None] + prior_weight)
    return posteriors, references
```

```python
import functools

import jax
import jax.numpy as jnp
from jax import lax
from jax.experimental import pallas as pl
from jax.experimental.pallas import tpu as pltpu
from jax.sharding import PartitionSpec as P

prior_weight = 1.0
very_low = -1e30
both = ("img", "ori")
lanes = 128
cores = 2
vmem = pl.BlockSpec(memory_space=pltpu.VMEM)
smem = pl.BlockSpec(memory_space=pltpu.SMEM)
anywhere = pl.BlockSpec(memory_space=pl.ANY)
contract_last = (((1,), (1,)), ((), ()))


def weighted_sums(weights, rows_block):
    return lax.dot_general(
        weights, rows_block, (((0,), (0,)), ((), ())), preferred_element_type=jnp.float32
    )


def reduced_body(images, precision, projections, tile_mask):
    lowered = images.astype(jnp.bfloat16)
    grouped = lax.all_gather(lowered, "ori", axis=0, tiled=True)
    proj_float = projections.astype(jnp.float32)
    squared = jnp.sum(proj_float * proj_float, axis=1)
    blocks, tiles_here = tile_mask.shape
    per_block = grouped.shape[0] // blocks
    tile_width = projections.shape[0] // tiles_here
    columns = grouped.shape[1]
    products = lax.dot_general(
        grouped, projections, contract_last, preferred_element_type=jnp.float32
    )
    scores = precision[:, None] * (products - 0.5 * squared[None, :])
    shaped = scores.reshape(blocks, per_block, tiles_here, tile_width)
    alive = jnp.broadcast_to((tile_mask > 0)[:, None, :, None], shaped.shape)
    masked = jnp.where(alive, shaped, very_low)
    local_high = jnp.max(masked, axis=(2, 3))
    row_high = lax.pmax(local_high, "ori")
    lifted = jnp.where(alive, jnp.exp(masked - row_high[:, :, None, None]), 0.0)
    row_total = lax.psum(jnp.sum(lifted, axis=(2, 3)), "ori")
    probable = lifted / row_total[:, :, None, None]
    posteriors = probable.reshape(scores.shape).astype(jnp.bfloat16)
    counts = jnp.sum(posteriors.astype(jnp.float32), axis=0)
    half_width = columns // 2
    halves = [
        lax.psum_scatter(
            weighted_sums(posteriors, part).astype(jnp.bfloat16),
            "img",
            scatter_dimension=0,
            tiled=True,
        ).astype(jnp.float32)
        for part in (grouped[:, :half_width], grouped[:, half_width:])
    ]
    totals = lax.psum_scatter(
        counts.astype(jnp.bfloat16), "img", scatter_dimension=0, tiled=True
    ).astype(jnp.float32)
    summed = jnp.concatenate(halves, axis=1)
    rows_here = summed.shape[0]
    first_row = lax.axis_index("img") * rows_here
    prior_rows = lax.dynamic_slice_in_dim(proj_float, first_row, rows_here, 0)
    refined = (summed + prior_weight * prior_rows) / (totals[:, None] + prior_weight)
    return (posteriors, refined)


def as_row(column):
    return jnp.transpose(jnp.broadcast_to(column, (column.shape[0], lanes)))[0:1, :]


def as_column(row):
    return jnp.transpose(jnp.broadcast_to(row, (lanes, row.shape[1])))[:, 0:1]


def scores_kernel(
    mask_s, prec_ref, own_ref, other_ref, proj_ref, scores_ref, stats_ref, half_ref,
    rows_buf, high, total, prec_col, sems,
):
    step = pl.program_id(0)
    here = lax.axis_index("ori")
    chip = lax.axis_index("img") // cores
    shard = own_ref.shape[0]
    blocks, tiles = mask_s.shape
    width = proj_ref.shape[0]
    tiles_here = tiles // pl.num_programs(0)
    tile = width // tiles_here

    @pl.when(step == 0)
    def _():
        copies = [
            pltpu.make_async_copy(
                ref, rows_buf.at[pl.ds(pl.multiple_of(at * shard, shard), shard)], sems.at[i]
            )
            for i, (ref, at) in enumerate(((own_ref, here), (other_ref, 1 - here)))
        ]
        for copy in copies:
            copy.start()
        prec_col[...] = jnp.transpose(
            jnp.broadcast_to(prec_ref[...], (lanes, prec_ref.shape[1]))
        )
        high[...] = jnp.full(high.shape, very_low, jnp.float32)
        total[...] = jnp.zeros(total.shape, jnp.float32)
        for copy in copies:
            copy.wait()

    wide = proj_ref[...].astype(jnp.float32)
    half = 0.5 * jnp.sum(wide * wide, axis=1, keepdims=True)
    half_wide = jnp.broadcast_to(half, (width, lanes))

    @pl.when(step == chip)
    def _():
        half_ref[...] = half_wide

    half_row = jnp.transpose(half_wide)[0:1, :]
    products = lax.dot_general(
        rows_buf[...], proj_ref[...], contract_last, preferred_element_type=jnp.float32
    )
    scores = prec_col[:, 0:1] * (products - half_row)
    for b in range(blocks):
        rows = slice(b * shard, (b + 1) * shard)
        parts = []
        for t in range(tiles_here):
            alive = mask_s[b, step * tiles_here + t] > 0
            kept = jnp.where(alive, scores[rows, t * tile : (t + 1) * tile], very_low)
            scores_ref[rows, t * tile : (t + 1) * tile] = kept
            parts += [kept[:, c : c + lanes] for c in range(0, tile, lanes)]
        before = high[rows, :]
        now = functools.reduce(jnp.maximum, parts, before)
        added = functools.reduce(jnp.add, [jnp.exp(part - now) for part in parts])
        total[rows, :] = total[rows, :] * jnp.exp(before - now) + added
        high[rows, :] = now

    @pl.when(step == pl.num_programs(0) - 1)
    def _():
        top = jnp.max(high[...], axis=1, keepdims=True)
        mass = jnp.sum(total[...] * jnp.exp(high[...] - top), axis=1, keepdims=True)
        stats_ref[0:1, :] = as_row(top)
        stats_ref[1:2, :] = as_row(mass)
        stats_ref[2:3, :] = prec_ref[...]
        stats_ref[3:8, :] = jnp.zeros((5, stats_ref.shape[1]), jnp.float32)


def posterior_kernel(scores_ref, mine_ref, theirs_ref, post_ref, meta_ref):
    top = jnp.maximum(mine_ref[0:1, :], theirs_ref[0:1, :])
    mass = mine_ref[1:2, :] * jnp.exp(mine_ref[0:1, :] - top) + theirs_ref[
        1:2, :
    ] * jnp.exp(theirs_ref[0:1, :] - top)
    share = 1.0 / mass

    @pl.when(pl.program_id(0) == 0)
    def _():
        parts, _, shard = meta_ref.shape
        for b in range(parts):
            columns = slice(b * shard, (b + 1) * shard)
            meta_ref[b, 0:1, :] = top[:, columns]
            meta_ref[b, 1:2, :] = share[:, columns]
            meta_ref[b, 2:8, :] = mine_ref[2:8, columns]

    post_ref[...] = (
        jnp.exp(scores_ref[...] - as_column(top)) * as_column(share)
    ).astype(post_ref.dtype)


def sums_kernel(steps, counts_of, first, last, *refs):
    mask_s, meta_ref, half_ref, proj_ref = refs[:4]
    refs = refs[4:]
    pieces = refs[: len(counts_of)]
    refs = refs[len(counts_of) :]
    if not first:
        acc_ref, cnt_ref = refs[:2]
        refs = refs[2:]
    outs, refs = refs[: 3 if last else 2], refs[3 if last else 2 :]
    proj_buf, rows_buf, weights_buf, seen_buf, sems = refs
    img, ori = lax.axis_index("img"), lax.axis_index("ori")
    chip, core = img // cores, lax.rem(img, cores)
    width, columns = proj_buf.shape
    shard = rows_buf.shape[0] // len(steps)
    copies = [
        pltpu.make_async_copy(
            proj_ref.at[pl.ds(pl.multiple_of(chip * width, width), width)],
            proj_buf,
            sems.at[len(pieces)],
        )
    ]
    at = 0
    for i, (piece, n) in enumerate(zip(pieces, counts_of, strict=True)):
        copies.append(pltpu.make_async_copy(piece, rows_buf.at[at : at + n], sems.at[i]))
        at += n
    for copy in copies:
        copy.start()
    for copy in copies:
        copy.wait()
    tiles = mask_s.shape[1]
    tiles_here = tiles * width // proj_ref.shape[0]
    tile = width // tiles_here
    products = lax.dot_general(
        proj_buf[...], rows_buf[...], contract_last, preferred_element_type=jnp.float32
    )
    weights, seen = [], jnp.zeros((width, shard), jnp.float32)
    for b, (d_img, d_ori) in enumerate(steps):
        source_img, source_ori = img ^ d_img, ori ^ d_ori
        parts = lax.div(mask_s.shape[0] * 1, lax.axis_size("img"))
        meta = meta_ref[lax.div(source_img, cores) * parts + source_ori]
        top, share, prec = meta[0:1, :], meta[1:2, :], meta[2:3, :]
        mine = prec * (products[:, b * shard : (b + 1) * shard] - half_ref[...])
        down = []
        for t in range(tiles_here):
            alive = mask_s[source_img * parts + source_ori, chip * tiles_here + t] > 0
            floor = jnp.where(alive, -top, very_low)
            down.append(
                (jnp.exp(mine[t * tile : (t + 1) * tile, :] + floor) * share).astype(
                    jnp.bfloat16
                )
            )
        weight = jnp.concatenate(down, axis=0)
        seen += weight.astype(jnp.float32)
        weights.append(weight)
    for b, weight in enumerate(weights):
        weights_buf[:, b * shard : (b + 1) * shard] = weight
    if not first:
        seen += cnt_ref[...]
    everything = pl.ds(0, width)
    if last:
        kept_ref, kept_cnt_ref, sent_ref = outs
        half_width = width // 2
        keep = pl.ds(pl.multiple_of(core * half_width, half_width), half_width)
        send = pl.ds(pl.multiple_of((1 - core) * half_width, half_width), half_width)
        seen_buf[...] = jnp.broadcast_to(jnp.sum(seen, axis=1, keepdims=True), seen.shape)
        kept_cnt_ref[...] = seen_buf[keep, :]
        sent_ref[:, columns:] = seen_buf[send, :].astype(jnp.bfloat16)
        targets = ((send, sent_ref), (keep, kept_ref))
    else:
        outs[1][...] = seen
        targets = ((everything, outs[0]),)
    chunk = min(columns, 512)
    for where, out in targets:
        for c in range(0, columns, chunk):
            part = slice(c, c + chunk)
            sums = lax.dot_general(
                weights_buf[where, :],
                rows_buf[:, part],
                (((1,), (0,)), ((), ())),
                preferred_element_type=jnp.float32,
            )
            if not first:
                sums += acc_ref[where, part]
            out[:, part] = sums.astype(out.dtype)


def final_kernel(kept_ref, kept_cnt_ref, got_ref, proj_ref, out_ref):
    columns = out_ref.shape[1]
    counts = kept_cnt_ref[:, 0:1] + got_ref[:, columns : columns + 1].astype(jnp.float32)
    sums = kept_ref[...] + got_ref[:, :columns].astype(jnp.float32)
    prior = prior_weight * proj_ref[...].astype(jnp.float32)
    out_ref[...] = (sums + prior) / (counts + prior_weight)


def gathered_body(n_img, n_ori, images, precision, projections, tile_mask):
    n = n_img * n_ori
    shard, columns = images.shape
    orient = projections.shape[0]
    chips = n_img // cores
    width = orient // chips
    blocks, tiles = tile_mask.shape

    def swap(a, d_img, d_ori):
        mask = d_img * n_ori + d_ori
        return lax.ppermute(a, both, [(i, i ^ mask) for i in range(n)])

    x, y, core = (0, 1), (cores, 0), (1, 0)
    lowered = images.astype(jnp.bfloat16)

    def plane(a):
        from_x, from_y = swap(a, *x), swap(a, *y)
        h = a.shape[0] // 2
        far = [swap(from_x[:h], *y), swap(from_y[h:], *x)]
        return [(x, [from_x]), (y, [from_y]), ((y[0], x[1]), far)]

    slabs = [(0, lowered)]
    bit = n_img // 2
    while bit > cores:
        slabs += [(d | bit, swap(a, bit, 0)) for d, a in slabs]
        bit //= 2
    order = sorted(slabs, key=lambda slab: slab[0].bit_count() * n_img + slab[0])
    groups = []
    for d, a in order:
        groups.append(
            [((d, 0), [a])] + [((d ^ p[0], p[1]), pieces) for p, pieces in plane(a)]
        )
    from_x = groups[0][1][1][0]

    all_masks = lax.all_gather(tile_mask, "img", axis=0, tiled=True)
    prec_row = precision.reshape(1, -1)
    rows = prec_row.shape[1]
    f32 = jnp.float32
    scores, stats, half = pl.pallas_call(
        scores_kernel,
        grid=(chips,),
        in_specs=[
            smem,
            vmem,
            anywhere,
            anywhere,
            pl.BlockSpec((width, columns), lambda i: (i, 0)),
        ],
        out_specs=[
            pl.BlockSpec((rows, width), lambda i: (0, i)),
            pl.BlockSpec((8, rows), lambda i: (0, 0)),
            pl.BlockSpec((width, lanes), lambda i: (0, 0)),
        ],
        out_shape=[
            jax.ShapeDtypeStruct((rows, orient), f32),
            jax.ShapeDtypeStruct((8, rows), f32),
            jax.ShapeDtypeStruct((width, lanes), f32),
        ],
        scratch_shapes=[
            pltpu.VMEM((rows, columns), jnp.bfloat16),
            pltpu.VMEM((rows, lanes), f32),
            pltpu.VMEM((rows, lanes), f32),
            pltpu.VMEM((rows, lanes), f32),
            pltpu.SemaphoreType.DMA((2,)),
        ],
        compiler_params=pltpu.CompilerParams(vmem_limit_bytes=32 * 2**20),
        cost_estimate=pl.CostEstimate(
            flops=2 * rows * orient * columns,
            bytes_accessed=2 * orient * columns + 4 * rows * orient,
            transcendentals=rows * orient,
        ),
        name="scores",
    )(tile_mask, prec_row, lowered, from_x, projections)
    theirs = swap(stats, *x)
    cut = 4
    posteriors, meta = pl.pallas_call(
        posterior_kernel,
        grid=(cut,),
        in_specs=[
            pl.BlockSpec((rows, orient // cut), lambda i: (0, i)),
            pl.BlockSpec((8, rows), lambda i: (0, 0)),
            pl.BlockSpec((8, rows), lambda i: (0, 0)),
        ],
        out_specs=[
            pl.BlockSpec((rows, orient // cut), lambda i: (0, i)),
            pl.BlockSpec((n_ori, 8, shard), lambda i: (0, 0, 0)),
        ],
        out_shape=[
            jax.ShapeDtypeStruct((rows, orient), jnp.bfloat16),
            jax.ShapeDtypeStruct((n_ori, 8, shard), f32),
        ],
        compiler_params=pltpu.CompilerParams(vmem_limit_bytes=32 * 2**20),
        cost_estimate=pl.CostEstimate(
            flops=3 * rows * orient,
            bytes_accessed=6 * rows * orient,
            transcendentals=rows * orient,
        ),
        name="posterior",
    )(scores, stats, theirs)
    same_core = [[i * cores + c for i in range(chips)] for c in range(cores)]
    all_meta = lax.all_gather(meta, "img", axis=0, tiled=True, axis_index_groups=same_core)

    def add(group, state, last):
        steps = tuple(d for d, _ in group)
        pieces = [p for _, ps in group for p in ps]
        counts_of = tuple(p.shape[0] for p in pieces)
        first = state is None
        images_here = sum(counts_of)
        if last:
            out_shape = [
                jax.ShapeDtypeStruct((width // 2, columns), f32),
                jax.ShapeDtypeStruct((width // 2, lanes), f32),
                jax.ShapeDtypeStruct((width // 2, columns + lanes), jnp.bfloat16),
            ]
            aliases = {}
        else:
            out_shape = [
                jax.ShapeDtypeStruct((width, columns), f32),
                jax.ShapeDtypeStruct((width, lanes), f32),
            ]
            aliases = {} if first else {4 + len(pieces): 0, 5 + len(pieces): 1}
        return pl.pallas_call(
            functools.partial(sums_kernel, steps, counts_of, first, last),
            in_specs=[smem, vmem, vmem, anywhere]
            + [anywhere] * len(pieces)
            + ([] if first else [vmem, vmem]),
            out_specs=[vmem] * len(out_shape),
            out_shape=out_shape,
            input_output_aliases=aliases,
            scratch_shapes=[
                pltpu.VMEM((width, columns), jnp.bfloat16),
                pltpu.VMEM((images_here, columns), jnp.bfloat16),
                pltpu.VMEM((width, images_here), jnp.bfloat16),
                pltpu.VMEM((width, lanes), f32),
                pltpu.SemaphoreType.DMA((len(pieces) + 1,)),
            ],
            compiler_params=pltpu.CompilerParams(vmem_limit_bytes=32 * 2**20),
            cost_estimate=pl.CostEstimate(
                flops=4 * width * images_here * columns,
                bytes_accessed=2 * (width + images_here) * columns + 8 * width * columns,
                transcendentals=width * images_here,
            ),
            name="sums",
        )(all_masks, all_meta, half, projections, *pieces, *(state or ()))

    state = None
    for i, group in enumerate(groups):
        state = add(group, state, i == len(groups) - 1)
    kept, kept_cnt, sent = state
    got = swap(sent, *core)
    out_rows = width // 2
    cut = 4
    first_row = lax.axis_index("img").astype(jnp.int32).reshape(1)
    refined = pl.pallas_call(
        lambda at, *refs: final_kernel(*refs),
        grid_spec=pltpu.PrefetchScalarGridSpec(
            num_scalar_prefetch=1,
            grid=(cut,),
            in_specs=[
                pl.BlockSpec((out_rows // cut, columns), lambda i, at: (i, 0)),
                pl.BlockSpec((out_rows // cut, lanes), lambda i, at: (i, 0)),
                pl.BlockSpec((out_rows // cut, columns + lanes), lambda i, at: (i, 0)),
                pl.BlockSpec((out_rows // cut, columns), lambda i, at: (at[0] * cut + i, 0)),
            ],
            out_specs=pl.BlockSpec((out_rows // cut, columns), lambda i, at: (i, 0)),
        ),
        out_shape=jax.ShapeDtypeStruct((out_rows, columns), f32),
        compiler_params=pltpu.CompilerParams(vmem_limit_bytes=32 * 2**20),
        name="final",
    )(first_row, kept, kept_cnt, got, projections)
    return posteriors, refined


def solution(mesh):
    n_img, n_ori = mesh.shape["img"], mesh.shape["ori"]

    def body(images, precision, projections, tile_mask):
        shard, columns = images.shape
        orient = projections.shape[0]
        blocks, tiles = tile_mask.shape
        gathered_bytes = 2 * images.size * n_img * n_ori // cores
        fits = (
            n_ori == 2
            and n_img >= 2 * cores
            and n_img & (n_img - 1) == 0
            and blocks == n_ori
            and shard % lanes == 0
            and tiles * cores % n_img == 0
            and orient % (tiles * lanes) == 0
            and gathered_bytes <= 16 * 2**20
        )
        if fits:
            return gathered_body(n_img, n_ori, images, precision, projections, tile_mask)
        return reduced_body(images, precision, projections, tile_mask)

    return jax.shard_map(
        body,
        mesh=mesh,
        in_specs=(P(("img", "ori"), None), P("img"), P("ori", None), P("img", "ori")),
        out_specs=(P("img", "ori"), P(("ori", "img"), None)),
        check_vma=False,
    )
```

```python
import functools

import jax
import jax.numpy as jnp
from jax import lax
from jax.experimental import pallas as pl
from jax.experimental.pallas import tpu as pltpu
from jax.sharding import PartitionSpec as P

prior_weight = 1.0
very_low = -1e30
both = ("img", "ori")
lanes = 128
cores = 2
vmem = pl.BlockSpec(memory_space=pltpu.VMEM)
smem = pl.BlockSpec(memory_space=pltpu.SMEM)
contract_last = (((1,), (1,)), ((), ()))


def weighted_sums(weights, rows_block):
    return lax.dot_general(
        weights, rows_block, (((0,), (0,)), ((), ())), preferred_element_type=jnp.float32
    )


def reduced_body(images, precision, projections, tile_mask):
    lowered = images.astype(jnp.bfloat16)
    grouped = lax.all_gather(lowered, "ori", axis=0, tiled=True)
    proj_float = projections.astype(jnp.float32)
    squared = jnp.sum(proj_float * proj_float, axis=1)
    blocks, tiles_here = tile_mask.shape
    per_block = grouped.shape[0] // blocks
    tile_width = projections.shape[0] // tiles_here
    columns = grouped.shape[1]
    products = lax.dot_general(
        grouped, projections, contract_last, preferred_element_type=jnp.float32
    )
    scores = precision[:, None] * (products - 0.5 * squared[None, :])
    shaped = scores.reshape(blocks, per_block, tiles_here, tile_width)
    alive = jnp.broadcast_to((tile_mask > 0)[:, None, :, None], shaped.shape)
    masked = jnp.where(alive, shaped, very_low)
    local_high = jnp.max(masked, axis=(2, 3))
    row_high = lax.pmax(local_high, "ori")
    lifted = jnp.where(alive, jnp.exp(masked - row_high[:, :, None, None]), 0.0)
    row_total = lax.psum(jnp.sum(lifted, axis=(2, 3)), "ori")
    probable = lifted / row_total[:, :, None, None]
    posteriors = probable.reshape(scores.shape).astype(jnp.bfloat16)
    counts = jnp.sum(posteriors.astype(jnp.float32), axis=0)
    half_width = columns // 2
    halves = [
        lax.psum_scatter(
            weighted_sums(posteriors, part).astype(jnp.bfloat16),
            "img",
            scatter_dimension=0,
            tiled=True,
        ).astype(jnp.float32)
        for part in (grouped[:, :half_width], grouped[:, half_width:])
    ]
    totals = lax.psum_scatter(
        counts.astype(jnp.bfloat16), "img", scatter_dimension=0, tiled=True
    ).astype(jnp.float32)
    summed = jnp.concatenate(halves, axis=1)
    rows_here = summed.shape[0]
    first_row = lax.axis_index("img") * rows_here
    prior_rows = lax.dynamic_slice_in_dim(proj_float, first_row, rows_here, 0)
    refined = (summed + prior_weight * prior_rows) / (totals[:, None] + prior_weight)
    return (posteriors, refined)


def as_row(column):
    return jnp.transpose(jnp.broadcast_to(column, (column.shape[0], lanes)))[0:1, :]


def as_column(row):
    return jnp.transpose(jnp.broadcast_to(row, (lanes, row.shape[1])))[:, 0:1]


def load_kernel(chips, away_ref, proj_ref, mine_ref, row_ref, col_ref, sems):
    width = proj_ref.shape[0] // chips
    chip = lax.axis_index("img") // cores

    def copy(i):
        rows = pl.ds(pl.multiple_of(i * width, width), width)
        return pltpu.make_async_copy(away_ref.at[rows], proj_ref.at[rows], sems.at[i])

    for i in range(chips):
        copy(i).start()
    mine = pltpu.make_async_copy(
        away_ref.at[pl.ds(pl.multiple_of(chip * width, width), width)], mine_ref, sems.at[chips]
    )
    mine.start()

    @pl.loop(0, chips)
    def _(i):
        copy(i).wait()
        here = pl.ds(pl.multiple_of(i * width, width), width)
        wide = proj_ref[here, :].astype(jnp.float32)
        half = 0.5 * jnp.sum(wide * wide, axis=1, keepdims=True)
        half_wide = jnp.broadcast_to(half, (width, lanes))
        row_ref[:, here] = jnp.transpose(half_wide)[0:8, :]

        @pl.when(i == chip)
        def _():
            col_ref[...] = half_wide

    mine.wait()


def scores_kernel(
    chips, mask_s, prec_ref, half_ref, own_ref, first_ref, second_ref, proj_ref, scores_ref, stats_ref,
    rows_buf,
):
    here = lax.axis_index("ori")
    core = lax.rem(lax.axis_index("img"), cores)
    shard = own_ref.shape[0]
    blocks, tiles = mask_s.shape
    width = proj_ref.shape[0] // chips
    tiles_here = tiles // chips
    tile = width // tiles_here
    rows_buf[pl.ds(pl.multiple_of(here * shard, shard), shard), :] = own_ref[...]
    there = pl.ds(pl.multiple_of((1 - here) * shard, shard), shard)

    @pl.when(core == 0)
    def _():
        rows_buf[there, :] = first_ref[...]

    @pl.when(core != 0)
    def _():
        rows_buf[there, :] = second_ref[...]

    prec_col = as_column(prec_ref[...])
    high = [jnp.full((shard, lanes), very_low, jnp.float32)] * blocks
    total = [jnp.zeros((shard, lanes), jnp.float32)] * blocks
    for step in range(chips):
        where = slice(step * width, (step + 1) * width)
        products = lax.dot_general(
            rows_buf[...], proj_ref[where, :], contract_last, preferred_element_type=jnp.float32
        )
        scores = prec_col * (products - half_ref[0:1, where])
        for b in range(blocks):
            rows = slice(b * shard, (b + 1) * shard)
            parts = []
            for t in range(tiles_here):
                at = step * width + t * tile
                alive = mask_s[b, step * tiles_here + t] > 0
                kept = jnp.where(alive, scores[rows, t * tile : (t + 1) * tile], very_low)
                scores_ref[rows, at : at + tile] = kept
                parts += [kept[:, c : c + lanes] for c in range(0, tile, lanes)]
            now = functools.reduce(jnp.maximum, parts, high[b])
            added = functools.reduce(jnp.add, [jnp.exp(part - now) for part in parts])
            total[b] = total[b] * jnp.exp(high[b] - now) + added
            high[b] = now
    for b in range(blocks):
        rows = slice(b * shard, (b + 1) * shard)
        top = jnp.max(high[b], axis=1, keepdims=True)
        mass = jnp.sum(total[b] * jnp.exp(high[b] - top), axis=1, keepdims=True)
        stats_ref[0:1, rows] = as_row(top)
        stats_ref[1:2, rows] = as_row(mass)
    stats_ref[2:8, :] = jnp.zeros((6, stats_ref.shape[1]), jnp.float32)


def joined(mine_ref, theirs_ref):
    top = jnp.maximum(mine_ref[0:1, :], theirs_ref[0:1, :])
    mass = mine_ref[1:2, :] * jnp.exp(mine_ref[0:1, :] - top) + theirs_ref[
        1:2, :
    ] * jnp.exp(theirs_ref[0:1, :] - top)
    return top, 1.0 / mass


def meta_kernel(mask_s, prec_ref, mine_ref, theirs_ref, meta_ref):
    top, share = joined(mine_ref, theirs_ref)
    parts, _, shard = meta_ref.shape
    tiles = mask_s.shape[1]
    for b in range(parts):
        columns = slice(b * shard, (b + 1) * shard)
        floor = -top[:, columns]
        for t in range(tiles):
            meta_ref[b, t : t + 1, :] = jnp.where(mask_s[b, t] > 0, floor, very_low)
        meta_ref[b, tiles : tiles + 1, :] = share[:, columns]
        meta_ref[b, tiles + 1 : tiles + 2, :] = prec_ref[:, columns]
        meta_ref[b, tiles + 2 : tiles + 8, :] = jnp.zeros((6, shard), jnp.float32)


def posterior_kernel(scores_ref, mine_ref, theirs_ref, post_ref):
    top, share = joined(mine_ref, theirs_ref)
    n = post_ref.shape[1]
    here = pl.ds(pl.multiple_of(pl.program_id(0) * n, n), n)
    post_ref[...] = (
        jnp.exp(scores_ref[:, here] - as_column(top)) * as_column(share)
    ).astype(post_ref.dtype)


def sums_kernel(n_metas, shapes, first, last, *refs):
    half_ref, proj_ref = refs[:2]
    metas, refs = refs[2 : 2 + n_metas], refs[2 + n_metas :]
    pieces, refs = refs[: len(shapes)], refs[len(shapes) :]
    if not first:
        acc_ref, cnt_ref = refs[:2]
        refs = refs[2:]
    n_outs = 3 if last else 2
    outs, (rows_buf, weights_buf, seen_buf) = refs[:n_outs], refs[n_outs:]
    img, ori = lax.axis_index("img"), lax.axis_index("ori")
    chip, core = img // cores, lax.rem(img, cores)
    width, columns = proj_ref.shape
    n_ori = lax.axis_size("ori")
    per_meta, tiles, shard = metas[0].shape
    tiles -= 8
    tiles_here = tiles * cores // lax.axis_size("img")
    tile = width // tiles_here
    seen = jnp.zeros((width, shard), jnp.float32)

    def meta_row(at, row):
        def read(d):
            which, inner = divmod(d[0] * n_ori, per_meta)
            return metas[which][inner + (ori ^ d[1]), pl.ds(row, 1), :]

        if at[0] == at[1]:
            return read(at[0])
        return jnp.where(core == 0, read(at[0]), read(at[1]))

    done = 0
    for piece, shards in zip(pieces, shapes, strict=True):
        n = piece.shape[0]
        rows_buf[done : done + n, :] = piece[...]
        done += n
    products = lax.dot_general(
        proj_ref[...], rows_buf[...], contract_last, preferred_element_type=jnp.float32
    )
    for b, at in enumerate(sum(shapes, ())):
        here = slice(b * shard, (b + 1) * shard)
        mine = meta_row(at, tiles + 1) * (products[:, here] - half_ref[...])
        share = meta_row(at, tiles)
        for t in range(tiles_here):
            down = slice(t * tile, (t + 1) * tile)
            floor = meta_row(at, chip * tiles_here + t)
            weights_buf[down, here] = (jnp.exp(mine[down, :] + floor) * share).astype(
                jnp.bfloat16
            )
        seen += weights_buf[:, here].astype(jnp.float32)
    if not first:
        seen += cnt_ref[...]
    if last:
        kept_ref, kept_cnt_ref, sent_ref = outs
        half_width = width // 2
        keep = pl.ds(pl.multiple_of(core * half_width, half_width), half_width)
        send = pl.ds(pl.multiple_of((1 - core) * half_width, half_width), half_width)
        seen_buf[...] = jnp.broadcast_to(jnp.sum(seen, axis=1, keepdims=True), seen.shape)
        kept_cnt_ref[...] = seen_buf[keep, :]
        sent_ref[:, columns:] = seen_buf[send, :].astype(jnp.bfloat16)
        targets = ((send, sent_ref), (keep, kept_ref))
    else:
        outs[1][...] = seen
        targets = ((pl.ds(0, width), outs[0]),)
    chunk = min(columns, 512)
    for where, out in targets:
        for c in range(0, columns, chunk):
            part = slice(c, c + chunk)
            sums = lax.dot_general(
                weights_buf[where, :],
                rows_buf[:, part],
                (((1,), (0,)), ((), ())),
                preferred_element_type=jnp.float32,
            )
            if not first:
                sums += acc_ref[where, part]
            out[:, part] = sums.astype(out.dtype)


def final_kernel(kept_ref, kept_cnt_ref, got_ref, proj_ref, out_ref):
    rows, columns = out_ref.shape
    core = lax.rem(lax.axis_index("img"), cores)
    first_row = (core * pl.num_programs(0) + pl.program_id(0)) * rows
    counts = kept_cnt_ref[:, 0:1] + got_ref[:, columns : columns + 1].astype(jnp.float32)
    sums = kept_ref[...] + got_ref[:, :columns].astype(jnp.float32)
    prior = prior_weight * proj_ref[pl.ds(pl.multiple_of(first_row, rows), rows), :].astype(
        jnp.float32
    )
    out_ref[...] = (sums + prior) * (1.0 / (counts + prior_weight))


def gathered_body(n_img, n_ori, images, precision, projections, tile_mask):
    n = n_img * n_ori
    shard, columns = images.shape
    orient = projections.shape[0]
    chips = n_img // cores
    width = orient // chips
    blocks, tiles = tile_mask.shape
    f32 = jnp.float32
    limit = pltpu.CompilerParams(vmem_limit_bytes=14 * 2**20)

    def swap(a, even, odd=None):
        masks = [d[0] * cores * n_ori + d[1] for d in (even, odd or even)]
        return lax.ppermute(a, both, [(i, i ^ masks[i // n_ori % cores]) for i in range(n)])

    def moved(shards, even, odd=None):
        odd = odd or even
        return tuple(
            ((e[0] ^ even[0], e[1] ^ even[1]), (o[0] ^ odd[0], o[1] ^ odd[1])) for e, o in shards
        )

    x, y = (0, 1), (1, 0)
    near, far = (x, y), (y, x)

    def sent(piece, even, odd=None):
        return moved(piece[0], even, odd), swap(piece[1], even, odd)

    def together(values):
        leaves, tree = jax.tree.flatten(values)
        arrays = iter(lax.optimization_barrier([a for a in leaves if not isinstance(a, int)]))
        return tree.unflatten([a if isinstance(a, int) else next(arrays) for a in leaves])

    lowered = images.astype(jnp.bfloat16)
    own = ((((0, 0), (0, 0)),), lowered)
    near_slab, far_slab = sent(own, (2, 0)), sent(own, (4, 0))
    own_a, own_b = sent(own, *near), sent(own, *far)

    prec_row = precision.reshape(1, -1)
    rows = prec_row.shape[1]
    held, held_chip, half_row, half_col = pl.pallas_call(
        functools.partial(load_kernel, chips),
        in_specs=[pl.BlockSpec(memory_space=pltpu.HBM)],
        out_specs=[vmem] * 4,
        out_shape=[
            pltpu.VMEM(projections.shape, projections.dtype),
            jax.ShapeDtypeStruct((width, columns), projections.dtype),
            jax.ShapeDtypeStruct((8, orient), f32),
            jax.ShapeDtypeStruct((width, lanes), f32),
        ],
        scratch_shapes=[pltpu.SemaphoreType.DMA((chips + 1,))],
        compiler_params=limit,
        cost_estimate=pl.CostEstimate(flops=0, bytes_accessed=0, transcendentals=0),
        name="load",
    )(pltpu.with_memory_space_constraint(projections, pltpu.HBM))
    held = pltpu.with_memory_space_constraint(held, pltpu.VMEM)
    own_a, own_b, held_chip, half_row, half_col = together(
        (own_a, own_b, held_chip, half_row, half_col)
    )
    own_c = sent(own_a, *far)
    whole = lambda i: (0, 0)
    scores, stats = pl.pallas_call(
        functools.partial(scores_kernel, chips),
        in_specs=[smem] + [vmem] * 6,
        out_specs=[vmem] * 2,
        out_shape=[
            pltpu.VMEM((rows, orient), f32),
            jax.ShapeDtypeStruct((8, rows), f32),
        ],
        scratch_shapes=[pltpu.VMEM((rows, columns), jnp.bfloat16)],
        compiler_params=limit,
        cost_estimate=pl.CostEstimate(flops=0, bytes_accessed=0, transcendentals=0),
        name="scores",
    )(tile_mask, prec_row, half_row, lowered, own_a[1], own_b[1], held)
    theirs = swap(stats, x)
    meta = pl.pallas_call(
        meta_kernel,
        in_specs=[smem, vmem, vmem, vmem],
        out_specs=vmem,
        out_shape=jax.ShapeDtypeStruct((n_ori, tiles + 8, shard), f32),
        compiler_params=limit,
        cost_estimate=pl.CostEstimate(flops=0, bytes_accessed=0, transcendentals=0),
        name="meta",
    )(tile_mask, prec_row, stats, theirs)
    close = [swap(meta, (d, 0)) for d in (1, 2, 3)]
    far_slab, near_slab, own_c, meta, scores = together(
        (far_slab, near_slab, own_c, meta, scores)
    )
    last_slab = sent(far_slab, (2, 0))
    far_a = sent(far_slab, *near)
    cut = 4
    posteriors = pl.pallas_call(
        posterior_kernel,
        grid=(cut,),
        in_specs=[
            vmem,
            pl.BlockSpec((8, rows), whole),
            pl.BlockSpec((8, rows), whole),
        ],
        out_specs=pl.BlockSpec((rows, orient // cut), lambda i: (0, i)),
        out_shape=jax.ShapeDtypeStruct((rows, orient), jnp.bfloat16),
        compiler_params=limit,
        cost_estimate=pl.CostEstimate(flops=0, bytes_accessed=0, transcendentals=0),
        name="posterior",
    )(scores, stats, theirs)

    close, posteriors, far_slab, near_slab = together(
        (close, posteriors, far_slab, near_slab)
    )
    far_b = sent(far_slab, *far)
    near_a = sent(near_slab, *near)
    metas = jnp.concatenate([meta, *close], axis=0)
    metas = [metas, swap(metas, (4, 0))]
    near_b = sent(own_b, (2, 0))
    far_a, far_b, last_slab = together((far_a, far_b, last_slab))
    far_c = sent(far_a, *far)
    last_a, last_b = sent(last_slab, *near), sent(last_slab, *far)

    def add(group, state, last):
        shapes = tuple(shards for shards, _ in group)
        pieces = [a for _, a in group]
        images_here = sum(a.shape[0] for a in pieces)
        first = state is None
        if last:
            out_shape = [
                jax.ShapeDtypeStruct((width // 2, columns), f32),
                jax.ShapeDtypeStruct((width // 2, lanes), f32),
                jax.ShapeDtypeStruct((width // 2, columns + lanes), jnp.bfloat16),
            ]
        else:
            out_shape = [
                jax.ShapeDtypeStruct((width, columns), f32),
                jax.ShapeDtypeStruct((width, lanes), f32),
            ]
        n_ins = 2 + len(metas) + len(pieces) + (0 if first else 2)
        return pl.pallas_call(
            functools.partial(sums_kernel, len(metas), shapes, first, last),
            in_specs=[vmem] * n_ins,
            out_specs=[vmem] * len(out_shape),
            out_shape=out_shape,
            input_output_aliases={} if first or last else {n_ins - 2: 0, n_ins - 1: 1},
            scratch_shapes=[
                pltpu.VMEM((images_here, columns), jnp.bfloat16),
                pltpu.VMEM((width, images_here), jnp.bfloat16),
                pltpu.VMEM((width, lanes), f32),
            ],
            compiler_params=limit,
        cost_estimate=pl.CostEstimate(flops=0, bytes_accessed=0, transcendentals=0),
            name="sums",
        )(half_col, held_chip, *metas, *pieces, *(state or ()))

    state = add([own, own_a, own_b, own_c], None, False)
    state = add([near_slab, far_slab, far_a, far_b], state, False)
    state, far_c, own_c = together((state, far_c, own_c))
    near_c = sent(own_c, (2, 0))
    state = add([near_a, far_c, last_slab], state, False)
    state, last_a = together((state, last_a))
    last_c = sent(last_a, *far)
    state = add([last_a, last_b, near_b], state, False)
    kept, kept_cnt, sent_away = add([near_c, last_c], state, True)
    got = lax.ppermute(sent_away, both, [(i, i ^ n_ori) for i in range(n)])
    out_rows = width // 2
    cut = 4
    refined = pl.pallas_call(
        final_kernel,
        grid=(cut,),
        in_specs=[
            pl.BlockSpec((out_rows // cut, columns), lambda i: (i, 0)),
            pl.BlockSpec((out_rows // cut, lanes), lambda i: (i, 0)),
            pl.BlockSpec((out_rows // cut, columns + lanes), lambda i: (i, 0)),
            vmem,
        ],
        out_specs=pl.BlockSpec((out_rows // cut, columns), lambda i: (i, 0)),
        out_shape=jax.ShapeDtypeStruct((out_rows, columns), f32),
        compiler_params=limit,
        cost_estimate=pl.CostEstimate(flops=0, bytes_accessed=0, transcendentals=0),
        name="final",
    )(kept, kept_cnt, got, held_chip)
    return posteriors, refined


def solution(mesh):
    n_img, n_ori = mesh.shape["img"], mesh.shape["ori"]

    def body(images, precision, projections, tile_mask):
        shard, columns = images.shape
        orient = projections.shape[0]
        blocks, tiles = tile_mask.shape
        gathered_bytes = 2 * images.size * n_img * n_ori // cores
        fits = (
            n_ori == 2
            and n_img == 8 * cores
            and blocks == n_ori
            and shard % lanes == 0
            and tiles * cores % n_img == 0
            and orient % (tiles * lanes) == 0
            and gathered_bytes <= 16 * 2**20
        )
        if fits:
            return gathered_body(n_img, n_ori, images, precision, projections, tile_mask)
        return reduced_body(images, precision, projections, tile_mask)

    return jax.shard_map(
        body,
        mesh=mesh,
        in_specs=(P(("img", "ori"), None), P("img"), P("ori", None), P("img", "ori")),
        out_specs=(P("img", "ori"), P(("ori", "img"), None)),
        check_vma=False,
    )
```

```python
import functools

import jax
import jax.numpy as jnp
from jax import lax
from jax.experimental import pallas as pl
from jax.experimental.pallas import tpu as pltpu
from jax.sharding import PartitionSpec as P

prior_weight = 1.0
very_low = -1e30
both = ("img", "ori")
lanes = 128
cores = 2
vmem = pl.BlockSpec(memory_space=pltpu.VMEM)
smem = pl.BlockSpec(memory_space=pltpu.SMEM)
contract_last = (((1,), (1,)), ((), ()))


def weighted_sums(weights, rows_block):
    return lax.dot_general(
        weights, rows_block, (((0,), (0,)), ((), ())), preferred_element_type=jnp.float32
    )


def reduced_body(images, precision, projections, tile_mask):
    lowered = images.astype(jnp.bfloat16)
    grouped = lax.all_gather(lowered, "ori", axis=0, tiled=True)
    proj_float = projections.astype(jnp.float32)
    squared = jnp.sum(proj_float * proj_float, axis=1)
    blocks, tiles_here = tile_mask.shape
    per_block = grouped.shape[0] // blocks
    tile_width = projections.shape[0] // tiles_here
    columns = grouped.shape[1]
    products = lax.dot_general(
        grouped, projections, contract_last, preferred_element_type=jnp.float32
    )
    scores = precision[:, None] * (products - 0.5 * squared[None, :])
    shaped = scores.reshape(blocks, per_block, tiles_here, tile_width)
    alive = jnp.broadcast_to((tile_mask > 0)[:, None, :, None], shaped.shape)
    masked = jnp.where(alive, shaped, very_low)
    local_high = jnp.max(masked, axis=(2, 3))
    row_high = lax.pmax(local_high, "ori")
    lifted = jnp.where(alive, jnp.exp(masked - row_high[:, :, None, None]), 0.0)
    row_total = lax.psum(jnp.sum(lifted, axis=(2, 3)), "ori")
    probable = lifted / row_total[:, :, None, None]
    posteriors = probable.reshape(scores.shape).astype(jnp.bfloat16)
    counts = jnp.sum(posteriors.astype(jnp.float32), axis=0)
    half_width = columns // 2
    halves = [
        lax.psum_scatter(
            weighted_sums(posteriors, part).astype(jnp.bfloat16),
            "img",
            scatter_dimension=0,
            tiled=True,
        ).astype(jnp.float32)
        for part in (grouped[:, :half_width], grouped[:, half_width:])
    ]
    totals = lax.psum_scatter(
        counts.astype(jnp.bfloat16), "img", scatter_dimension=0, tiled=True
    ).astype(jnp.float32)
    summed = jnp.concatenate(halves, axis=1)
    rows_here = summed.shape[0]
    first_row = lax.axis_index("img") * rows_here
    prior_rows = lax.dynamic_slice_in_dim(proj_float, first_row, rows_here, 0)
    refined = (summed + prior_weight * prior_rows) / (totals[:, None] + prior_weight)
    return (posteriors, refined)


def as_row(column):
    return jnp.transpose(jnp.broadcast_to(column, (column.shape[0], lanes)))[0:1, :]


def as_column(row):
    return jnp.transpose(jnp.broadcast_to(row, (lanes, row.shape[1])))[:, 0:1]


def load_kernel(chips, away_ref, proj_ref, mine_ref, row_ref, col_ref, sems):
    width = proj_ref.shape[0] // chips
    chip = lax.axis_index("img") // cores

    def copy(i):
        rows = pl.ds(pl.multiple_of(i * width, width), width)
        return pltpu.make_async_copy(away_ref.at[rows], proj_ref.at[rows], sems.at[i])

    for i in range(chips):
        copy(i).start()
    mine = pltpu.make_async_copy(
        away_ref.at[pl.ds(pl.multiple_of(chip * width, width), width)], mine_ref, sems.at[chips]
    )
    mine.start()

    @pl.loop(0, chips)
    def _(i):
        copy(i).wait()
        here = pl.ds(pl.multiple_of(i * width, width), width)
        wide = proj_ref[here, :].astype(jnp.float32)
        half = 0.5 * jnp.sum(wide * wide, axis=1, keepdims=True)
        half_wide = jnp.broadcast_to(half, (width, lanes))
        row_ref[:, here] = jnp.transpose(half_wide)[0:8, :]

        @pl.when(i == chip)
        def _():
            col_ref[...] = half_wide

    mine.wait()


def scores_kernel(
    chips, mask_s, prec_ref, half_ref, own_ref, first_ref, second_ref, proj_ref, scores_ref, stats_ref,
    rows_buf,
):
    here = lax.axis_index("ori")
    core = lax.rem(lax.axis_index("img"), cores)
    shard = own_ref.shape[0]
    blocks, tiles = mask_s.shape
    width = proj_ref.shape[0] // chips
    tiles_here = tiles // chips
    tile = width // tiles_here
    rows_buf[pl.ds(pl.multiple_of(here * shard, shard), shard), :] = own_ref[...]
    there = pl.ds(pl.multiple_of((1 - here) * shard, shard), shard)

    @pl.when(core == 0)
    def _():
        rows_buf[there, :] = first_ref[...]

    @pl.when(core != 0)
    def _():
        rows_buf[there, :] = second_ref[...]

    prec_col = as_column(prec_ref[...])
    high = [jnp.full((shard, lanes), very_low, jnp.float32)] * blocks
    total = [jnp.zeros((shard, lanes), jnp.float32)] * blocks
    for step in range(chips):
        where = slice(step * width, (step + 1) * width)
        products = lax.dot_general(
            rows_buf[...], proj_ref[where, :], contract_last, preferred_element_type=jnp.float32
        )
        scores = prec_col * (products - half_ref[0:1, where])
        for b in range(blocks):
            rows = slice(b * shard, (b + 1) * shard)
            parts = []
            for t in range(tiles_here):
                at = step * width + t * tile
                alive = mask_s[b, step * tiles_here + t] > 0
                kept = jnp.where(alive, scores[rows, t * tile : (t + 1) * tile], very_low)
                scores_ref[rows, at : at + tile] = kept
                parts += [kept[:, c : c + lanes] for c in range(0, tile, lanes)]
            now = functools.reduce(jnp.maximum, parts, high[b])
            added = functools.reduce(jnp.add, [jnp.exp(part - now) for part in parts])
            total[b] = total[b] * jnp.exp(high[b] - now) + added
            high[b] = now
    for b in range(blocks):
        rows = slice(b * shard, (b + 1) * shard)
        top = jnp.max(high[b], axis=1, keepdims=True)
        mass = jnp.sum(total[b] * jnp.exp(high[b] - top), axis=1, keepdims=True)
        stats_ref[0:1, rows] = as_row(top)
        stats_ref[1:2, rows] = as_row(mass)
    stats_ref[2:8, :] = jnp.zeros((6, stats_ref.shape[1]), jnp.float32)


def joined(mine_ref, theirs_ref):
    top = jnp.maximum(mine_ref[0:1, :], theirs_ref[0:1, :])
    mass = mine_ref[1:2, :] * jnp.exp(mine_ref[0:1, :] - top) + theirs_ref[
        1:2, :
    ] * jnp.exp(theirs_ref[0:1, :] - top)
    return top, 1.0 / mass


def meta_kernel(mask_s, prec_ref, mine_ref, theirs_ref, meta_ref):
    top, share = joined(mine_ref, theirs_ref)
    parts, _, shard = meta_ref.shape
    tiles = mask_s.shape[1]
    at = lax.broadcasted_iota(jnp.int32, (1, shard), 1)
    for b in range(parts):
        columns = slice(b * shard, (b + 1) * shard)
        meta_ref[b, 0:1, :] = top[:, columns]
        meta_ref[b, 1:2, :] = share[:, columns]
        meta_ref[b, 2:3, :] = prec_ref[:, columns]
        may = jnp.zeros((1, shard), jnp.float32)
        for t in range(tiles):
            may = jnp.where((at == t) & (mask_s[b, t] > 0), 1.0, may)
        meta_ref[b, 3:4, :] = may
        meta_ref[b, 4:8, :] = jnp.zeros((4, shard), jnp.float32)


def posterior_kernel(scores_ref, mine_ref, theirs_ref, post_ref):
    top, share = joined(mine_ref, theirs_ref)
    n = post_ref.shape[1]
    here = pl.ds(pl.multiple_of(pl.program_id(0) * n, n), n)
    post_ref[...] = (
        jnp.exp(scores_ref[:, here] - as_column(top)) * as_column(share)
    ).astype(post_ref.dtype)


def sums_kernel(n_metas, tiles_here, shapes, first, last, *refs):
    half_ref, proj_ref = refs[:2]
    metas, refs = refs[2 : 2 + n_metas], refs[2 + n_metas :]
    pieces, refs = refs[: len(shapes)], refs[len(shapes) :]
    if not first:
        acc_ref, cnt_ref = refs[:2]
        refs = refs[2:]
    n_outs = 3 if last else 2
    outs, (rows_buf, weights_buf, seen_buf) = refs[:n_outs], refs[n_outs:]
    img, ori = lax.axis_index("img"), lax.axis_index("ori")
    chip, core = img // cores, lax.rem(img, cores)
    width, columns = proj_ref.shape
    n_ori = lax.axis_size("ori")
    per_meta, _, shard = metas[0].shape
    tile = width // tiles_here
    seen = jnp.zeros((width, shard), jnp.float32)
    lane = lax.broadcasted_iota(jnp.int32, (1, shard), 1)

    def meta_row(at, row):
        def read(d):
            which, inner = divmod(d[0] * n_ori, per_meta)
            return metas[which][inner + (ori ^ d[1]), pl.ds(row, 1), :]

        if at[0] == at[1]:
            return read(at[0])
        return jnp.where(core == 0, read(at[0]), read(at[1]))

    done = 0
    for piece, shards in zip(pieces, shapes, strict=True):
        n = piece.shape[0]
        rows_buf[done : done + n, :] = piece[...]
        done += n
    products = lax.dot_general(
        proj_ref[...], rows_buf[...], contract_last, preferred_element_type=jnp.float32
    )
    for b, at in enumerate(sum(shapes, ())):
        here = slice(b * shard, (b + 1) * shard)
        top, share, prec, may = (meta_row(at, row) for row in range(4))
        mine = prec * (products[:, here] - half_ref[...])
        for t in range(tiles_here):
            down = slice(t * tile, (t + 1) * tile)
            mark = jnp.where(lane == chip * tiles_here + t, may, 0.0)
            floor = jnp.where(jnp.max(mark, axis=1, keepdims=True) > 0, -top, very_low)
            weights_buf[down, here] = (jnp.exp(mine[down, :] + floor) * share).astype(
                jnp.bfloat16
            )
        seen += weights_buf[:, here].astype(jnp.float32)
    if not first:
        seen += cnt_ref[...]
    if last:
        kept_ref, kept_cnt_ref, sent_ref = outs
        half_width = width // 2
        keep = pl.ds(pl.multiple_of(core * half_width, half_width), half_width)
        send = pl.ds(pl.multiple_of((1 - core) * half_width, half_width), half_width)
        seen_buf[...] = jnp.broadcast_to(jnp.sum(seen, axis=1, keepdims=True), seen.shape)
        kept_cnt_ref[...] = seen_buf[keep, :]
        sent_ref[:, columns:] = seen_buf[send, :].astype(jnp.bfloat16)
        targets = ((send, sent_ref), (keep, kept_ref))
    else:
        outs[1][...] = seen
        targets = ((pl.ds(0, width), outs[0]),)
    chunk = min(columns, 512)
    for where, out in targets:
        for c in range(0, columns, chunk):
            part = slice(c, c + chunk)
            sums = lax.dot_general(
                weights_buf[where, :],
                rows_buf[:, part],
                (((1,), (0,)), ((), ())),
                preferred_element_type=jnp.float32,
            )
            if not first:
                sums += acc_ref[where, part]
            out[:, part] = sums.astype(out.dtype)


def final_kernel(kept_ref, kept_cnt_ref, got_ref, proj_ref, out_ref):
    rows, columns = out_ref.shape
    core = lax.rem(lax.axis_index("img"), cores)
    here = pl.ds(pl.multiple_of(pl.program_id(0) * rows, rows), rows)
    first_row = (core * pl.num_programs(0) + pl.program_id(0)) * rows
    counts = kept_cnt_ref[here, 0:1] + got_ref[here, columns : columns + 1].astype(jnp.float32)
    sums = kept_ref[here, :] + got_ref[here, :columns].astype(jnp.float32)
    prior = prior_weight * proj_ref[pl.ds(pl.multiple_of(first_row, rows), rows), :].astype(
        jnp.float32
    )
    out_ref[...] = (sums + prior) * (1.0 / (counts + prior_weight))


def gathered_body(n_img, n_ori, images, precision, projections, tile_mask):
    n = n_img * n_ori
    shard, columns = images.shape
    orient = projections.shape[0]
    chips = n_img // cores
    width = orient // chips
    blocks, tiles = tile_mask.shape
    f32 = jnp.float32
    limit = pltpu.CompilerParams(vmem_limit_bytes=14 * 2**20)

    def swap(a, even, odd=None):
        masks = [d[0] * cores * n_ori + d[1] for d in (even, odd or even)]
        return lax.ppermute(a, both, [(i, i ^ masks[i // n_ori % cores]) for i in range(n)])

    def moved(shards, even, odd=None):
        odd = odd or even
        return tuple(
            ((e[0] ^ even[0], e[1] ^ even[1]), (o[0] ^ odd[0], o[1] ^ odd[1])) for e, o in shards
        )

    x, y = (0, 1), (1, 0)
    near, far = (x, y), (y, x)

    def sent(piece, even, odd=None):
        return moved(piece[0], even, odd), swap(piece[1], even, odd)

    def together(values):
        leaves, tree = jax.tree.flatten(values)
        arrays = iter(lax.optimization_barrier([a for a in leaves if not isinstance(a, int)]))
        return tree.unflatten([a if isinstance(a, int) else next(arrays) for a in leaves])

    lowered = images.astype(jnp.bfloat16)
    own = ((((0, 0), (0, 0)),), lowered)
    near_slab, far_slab = sent(own, (2, 0)), sent(own, (4, 0))
    own_a, own_b = sent(own, *near), sent(own, *far)

    prec_row = precision.reshape(1, -1)
    rows = prec_row.shape[1]
    held, held_chip, half_row, half_col = pl.pallas_call(
        functools.partial(load_kernel, chips),
        in_specs=[pl.BlockSpec(memory_space=pltpu.HBM)],
        out_specs=[vmem] * 4,
        out_shape=[
            pltpu.VMEM(projections.shape, projections.dtype),
            jax.ShapeDtypeStruct((width, columns), projections.dtype),
            jax.ShapeDtypeStruct((8, orient), f32),
            jax.ShapeDtypeStruct((width, lanes), f32),
        ],
        scratch_shapes=[pltpu.SemaphoreType.DMA((chips + 1,))],
        compiler_params=limit,
        cost_estimate=pl.CostEstimate(flops=0, bytes_accessed=0, transcendentals=0),
        name="load",
    )(pltpu.with_memory_space_constraint(projections, pltpu.HBM))
    held = pltpu.with_memory_space_constraint(held, pltpu.VMEM)
    own_a, own_b, held_chip, half_row, half_col = together(
        (own_a, own_b, held_chip, half_row, half_col)
    )
    own_c = sent(own_a, *far)
    whole = lambda i: (0, 0)
    scores, stats = pl.pallas_call(
        functools.partial(scores_kernel, chips),
        in_specs=[smem] + [vmem] * 6,
        out_specs=[vmem] * 2,
        out_shape=[
            pltpu.VMEM((rows, orient), f32),
            jax.ShapeDtypeStruct((8, rows), f32),
        ],
        scratch_shapes=[pltpu.VMEM((rows, columns), jnp.bfloat16)],
        compiler_params=limit,
        cost_estimate=pl.CostEstimate(flops=0, bytes_accessed=0, transcendentals=0),
        name="scores",
    )(tile_mask, prec_row, half_row, lowered, own_a[1], own_b[1], held)
    theirs = swap(stats, x)
    meta = pl.pallas_call(
        meta_kernel,
        in_specs=[smem, vmem, vmem, vmem],
        out_specs=vmem,
        out_shape=jax.ShapeDtypeStruct((n_ori, 8, shard), f32),
        compiler_params=limit,
        cost_estimate=pl.CostEstimate(flops=0, bytes_accessed=0, transcendentals=0),
        name="meta",
    )(tile_mask, prec_row, stats, theirs)
    close = [swap(meta, (d, 0)) for d in (1, 2, 3)]
    far_slab, near_slab, own_c, meta, scores = together(
        (far_slab, near_slab, own_c, meta, scores)
    )
    last_slab = sent(far_slab, (2, 0))
    far_a = sent(far_slab, *near)
    cut = 4
    posteriors = pl.pallas_call(
        posterior_kernel,
        grid=(cut,),
        in_specs=[
            vmem,
            pl.BlockSpec((8, rows), whole),
            pl.BlockSpec((8, rows), whole),
        ],
        out_specs=pl.BlockSpec((rows, orient // cut), lambda i: (0, i)),
        out_shape=jax.ShapeDtypeStruct((rows, orient), jnp.bfloat16),
        compiler_params=limit,
        cost_estimate=pl.CostEstimate(flops=0, bytes_accessed=0, transcendentals=0),
        name="posterior",
    )(scores, stats, theirs)

    close, posteriors, far_slab, near_slab = together(
        (close, posteriors, far_slab, near_slab)
    )
    far_b = sent(far_slab, *far)
    metas = jnp.concatenate([meta, *close], axis=0)
    metas = [metas, swap(metas, (4, 0))]
    far_a, far_b, last_slab, metas, own_b, own_c = together(
        (far_a, far_b, last_slab, metas, own_b, own_c)
    )
    far_c = sent(far_a, *far)
    last_a, last_b = sent(last_slab, *near), sent(last_slab, *far)
    near_b, near_c = sent(own_b, (2, 0)), sent(own_c, (2, 0))

    def add(group, state, last):
        shapes = tuple(shards for shards, _ in group)
        pieces = [a for _, a in group]
        images_here = sum(a.shape[0] for a in pieces)
        first = state is None
        if last:
            out_shape = [
                jax.ShapeDtypeStruct((width // 2, columns), f32),
                jax.ShapeDtypeStruct((width // 2, lanes), f32),
                jax.ShapeDtypeStruct((width // 2, columns + lanes), jnp.bfloat16),
            ]
        else:
            out_shape = [
                jax.ShapeDtypeStruct((width, columns), f32),
                jax.ShapeDtypeStruct((width, lanes), f32),
            ]
        n_ins = 2 + len(metas) + len(pieces) + (0 if first else 2)
        return pl.pallas_call(
            functools.partial(sums_kernel, len(metas), tiles * cores // n_img, shapes, first, last),
            in_specs=[vmem] * n_ins,
            out_specs=[vmem] * len(out_shape),
            out_shape=out_shape,
            input_output_aliases={} if first or last else {n_ins - 2: 0, n_ins - 1: 1},
            scratch_shapes=[
                pltpu.VMEM((images_here, columns), jnp.bfloat16),
                pltpu.VMEM((width, images_here), jnp.bfloat16),
                pltpu.VMEM((width, lanes), f32),
            ],
            compiler_params=limit,
        cost_estimate=pl.CostEstimate(flops=0, bytes_accessed=0, transcendentals=0),
            name="sums",
        )(half_col, held_chip, *metas, *pieces, *(state or ()))

    state = add([own, own_a, own_b, own_c], None, False)
    state = add([near_slab, far_slab, far_a, far_b], state, False)
    state, near_slab, far_c, last_a = together((state, near_slab, far_c, last_a))
    last_c = sent(last_a, *far)
    near_a = sent(near_slab, *near)
    state = add([far_c, last_slab, last_a], state, False)
    state, last_b, near_b = together((state, last_b, near_b))
    state = add([last_b, near_b], state, False)
    kept, kept_cnt, sent_away = add([near_a, near_c, last_c], state, True)
    got = lax.ppermute(sent_away, both, [(i, i ^ n_ori) for i in range(n)])
    out_rows = width // 2
    cut = 4
    refined = pl.pallas_call(
        final_kernel,
        grid=(cut,),
        in_specs=[vmem] * 4,
        out_specs=pl.BlockSpec((out_rows // cut, columns), lambda i: (i, 0)),
        out_shape=jax.ShapeDtypeStruct((out_rows, columns), f32),
        compiler_params=limit,
        cost_estimate=pl.CostEstimate(flops=0, bytes_accessed=0, transcendentals=0),
        name="final",
    )(kept, kept_cnt, got, held_chip)
    return posteriors, refined


def solution(mesh):
    n_img, n_ori = mesh.shape["img"], mesh.shape["ori"]

    def body(images, precision, projections, tile_mask):
        shard, columns = images.shape
        orient = projections.shape[0]
        blocks, tiles = tile_mask.shape
        gathered_bytes = 2 * images.size * n_img * n_ori // cores
        fits = (
            n_ori == 2
            and n_img == 8 * cores
            and blocks == n_ori
            and shard % lanes == 0
            and tiles * cores % n_img == 0
            and orient % (tiles * lanes) == 0
            and tiles <= shard
            and gathered_bytes <= 16 * 2**20
        )
        if fits:
            return gathered_body(n_img, n_ori, images, precision, projections, tile_mask)
        return reduced_body(images, precision, projections, tile_mask)

    return jax.shard_map(
        body,
        mesh=mesh,
        in_specs=(P(("img", "ori"), None), P("img"), P("ori", None), P("img", "ori")),
        out_specs=(P("img", "ori"), P(("ori", "img"), None)),
        check_vma=False,
    )
```

```python
import functools

import jax
import jax.numpy as jnp
from jax import lax
from jax.experimental import pallas as pl
from jax.experimental.pallas import tpu as pltpu
from jax.sharding import PartitionSpec as P

prior_weight = 1.0
very_low = -1e30
both = ("img", "ori")
lanes = 128
cores = 2
vmem = pl.BlockSpec(memory_space=pltpu.VMEM)
smem = pl.BlockSpec(memory_space=pltpu.SMEM)
contract_last = (((1,), (1,)), ((), ()))


def weighted_sums(weights, rows_block):
    return lax.dot_general(
        weights, rows_block, (((0,), (0,)), ((), ())), preferred_element_type=jnp.float32
    )


def reduced_body(images, precision, projections, tile_mask):
    lowered = images.astype(jnp.bfloat16)
    grouped = lax.all_gather(lowered, "ori", axis=0, tiled=True)
    proj_float = projections.astype(jnp.float32)
    squared = jnp.sum(proj_float * proj_float, axis=1)
    blocks, tiles_here = tile_mask.shape
    per_block = grouped.shape[0] // blocks
    tile_width = projections.shape[0] // tiles_here
    columns = grouped.shape[1]
    products = lax.dot_general(
        grouped, projections, contract_last, preferred_element_type=jnp.float32
    )
    scores = precision[:, None] * (products - 0.5 * squared[None, :])
    shaped = scores.reshape(blocks, per_block, tiles_here, tile_width)
    alive = jnp.broadcast_to((tile_mask > 0)[:, None, :, None], shaped.shape)
    masked = jnp.where(alive, shaped, very_low)
    local_high = jnp.max(masked, axis=(2, 3))
    row_high = lax.pmax(local_high, "ori")
    lifted = jnp.where(alive, jnp.exp(masked - row_high[:, :, None, None]), 0.0)
    row_total = lax.psum(jnp.sum(lifted, axis=(2, 3)), "ori")
    probable = lifted / row_total[:, :, None, None]
    posteriors = probable.reshape(scores.shape).astype(jnp.bfloat16)
    counts = jnp.sum(posteriors.astype(jnp.float32), axis=0)
    half_width = columns // 2
    halves = [
        lax.psum_scatter(
            weighted_sums(posteriors, part).astype(jnp.bfloat16),
            "img",
            scatter_dimension=0,
            tiled=True,
        ).astype(jnp.float32)
        for part in (grouped[:, :half_width], grouped[:, half_width:])
    ]
    totals = lax.psum_scatter(
        counts.astype(jnp.bfloat16), "img", scatter_dimension=0, tiled=True
    ).astype(jnp.float32)
    summed = jnp.concatenate(halves, axis=1)
    rows_here = summed.shape[0]
    first_row = lax.axis_index("img") * rows_here
    prior_rows = lax.dynamic_slice_in_dim(proj_float, first_row, rows_here, 0)
    refined = (summed + prior_weight * prior_rows) / (totals[:, None] + prior_weight)
    return (posteriors, refined)


def as_row(column):
    return jnp.transpose(jnp.broadcast_to(column, (column.shape[0], lanes)))[0:1, :]


def as_column(row):
    return jnp.transpose(jnp.broadcast_to(row, (lanes, row.shape[1])))[:, 0:1]


def load_kernel(chips, away_ref, proj_ref, mine_ref, row_ref, col_ref, sems):
    width = proj_ref.shape[0] // chips
    chip = lax.axis_index("img") // cores

    def copy(i):
        rows = pl.ds(pl.multiple_of(i * width, width), width)
        return pltpu.make_async_copy(away_ref.at[rows], proj_ref.at[rows], sems.at[i])

    for i in range(chips):
        copy(i).start()
    mine = pltpu.make_async_copy(
        away_ref.at[pl.ds(pl.multiple_of(chip * width, width), width)], mine_ref, sems.at[chips]
    )
    mine.start()

    @pl.loop(0, chips)
    def _(i):
        copy(i).wait()
        here = pl.ds(pl.multiple_of(i * width, width), width)
        wide = proj_ref[here, :].astype(jnp.float32)
        half = 0.5 * jnp.sum(wide * wide, axis=1, keepdims=True)
        half_wide = jnp.broadcast_to(half, (width, lanes))
        row_ref[:, here] = jnp.transpose(half_wide)[0:8, :]

        @pl.when(i == chip)
        def _():
            col_ref[...] = half_wide

    mine.wait()


def scores_kernel(
    chips, mask_s, prec_ref, half_ref, own_ref, first_ref, second_ref, proj_ref, scores_ref, stats_ref,
    rows_buf,
):
    here = lax.axis_index("ori")
    core = lax.rem(lax.axis_index("img"), cores)
    shard = own_ref.shape[0]
    blocks, tiles = mask_s.shape
    width = proj_ref.shape[0] // chips
    tiles_here = tiles // chips
    tile = width // tiles_here
    rows_buf[pl.ds(pl.multiple_of(here * shard, shard), shard), :] = own_ref[...]
    there = pl.ds(pl.multiple_of((1 - here) * shard, shard), shard)

    @pl.when(core == 0)
    def _():
        rows_buf[there, :] = first_ref[...]

    @pl.when(core != 0)
    def _():
        rows_buf[there, :] = second_ref[...]

    prec_col = as_column(prec_ref[...])
    high = [jnp.full((shard, lanes), very_low, jnp.float32)] * blocks
    total = [jnp.zeros((shard, lanes), jnp.float32)] * blocks
    for step in range(chips):
        where = slice(step * width, (step + 1) * width)
        products = lax.dot_general(
            rows_buf[...], proj_ref[where, :], contract_last, preferred_element_type=jnp.float32
        )
        scores = prec_col * (products - half_ref[0:1, where])
        for b in range(blocks):
            rows = slice(b * shard, (b + 1) * shard)
            parts = []
            for t in range(tiles_here):
                at = step * width + t * tile
                alive = mask_s[b, step * tiles_here + t] > 0
                kept = jnp.where(alive, scores[rows, t * tile : (t + 1) * tile], very_low)
                scores_ref[rows, at : at + tile] = kept
                parts += [kept[:, c : c + lanes] for c in range(0, tile, lanes)]
            now = functools.reduce(jnp.maximum, parts, high[b])
            added = functools.reduce(jnp.add, [jnp.exp(part - now) for part in parts])
            total[b] = total[b] * jnp.exp(high[b] - now) + added
            high[b] = now
    for b in range(blocks):
        rows = slice(b * shard, (b + 1) * shard)
        top = jnp.max(high[b], axis=1, keepdims=True)
        mass = jnp.sum(total[b] * jnp.exp(high[b] - top), axis=1, keepdims=True)
        stats_ref[0:1, rows] = as_row(top)
        stats_ref[1:2, rows] = as_row(mass)
    stats_ref[2:8, :] = jnp.zeros((6, stats_ref.shape[1]), jnp.float32)


def joined(mine_ref, theirs_ref):
    top = jnp.maximum(mine_ref[0:1, :], theirs_ref[0:1, :])
    mass = mine_ref[1:2, :] * jnp.exp(mine_ref[0:1, :] - top) + theirs_ref[
        1:2, :
    ] * jnp.exp(theirs_ref[0:1, :] - top)
    return top, 1.0 / mass


def meta_kernel(mask_s, prec_ref, mine_ref, theirs_ref, meta_ref):
    top, share = joined(mine_ref, theirs_ref)
    parts, _, shard = meta_ref.shape
    tiles = mask_s.shape[1]
    at = lax.broadcasted_iota(jnp.int32, (1, shard), 1)
    for b in range(parts):
        columns = slice(b * shard, (b + 1) * shard)
        meta_ref[b, 0:1, :] = top[:, columns]
        meta_ref[b, 1:2, :] = share[:, columns]
        meta_ref[b, 2:3, :] = prec_ref[:, columns]
        may = jnp.zeros((1, shard), jnp.float32)
        for t in range(tiles):
            may = jnp.where((at == t) & (mask_s[b, t] > 0), 1.0, may)
        meta_ref[b, 3:4, :] = may
        meta_ref[b, 4:8, :] = jnp.zeros((4, shard), jnp.float32)


def posterior_kernel(scores_ref, mine_ref, theirs_ref, post_ref):
    top, share = joined(mine_ref, theirs_ref)
    n = post_ref.shape[1]
    here = pl.ds(pl.multiple_of(pl.program_id(0) * n, n), n)
    post_ref[...] = (
        jnp.exp(scores_ref[:, here] - as_column(top)) * as_column(share)
    ).astype(post_ref.dtype)


def sums_kernel(n_metas, tiles_here, shapes, first, last, *refs):
    half_ref, proj_ref = refs[:2]
    metas, refs = refs[2 : 2 + n_metas], refs[2 + n_metas :]
    pieces, refs = refs[: len(shapes)], refs[len(shapes) :]
    if not first:
        acc_ref, cnt_ref = refs[:2]
        refs = refs[2:]
    n_outs = 3 if last else 2
    outs, (rows_buf, weights_buf, seen_buf) = refs[:n_outs], refs[n_outs:]
    img, ori = lax.axis_index("img"), lax.axis_index("ori")
    chip, core = img // cores, lax.rem(img, cores)
    width, columns = proj_ref.shape
    n_ori = lax.axis_size("ori")
    per_meta, _, shard = metas[0].shape
    tile = width // tiles_here
    seen = jnp.zeros((width, shard), jnp.float32)
    lane = lax.broadcasted_iota(jnp.int32, (1, shard), 1)

    def meta_row(at, row):
        def read(d):
            which, inner = divmod(d[0] * n_ori, per_meta)
            return metas[which][inner + (ori ^ d[1]), pl.ds(row, 1), :]

        if at[0] == at[1]:
            return read(at[0])
        return jnp.where(core == 0, read(at[0]), read(at[1]))

    done = 0
    for piece, shards in zip(pieces, shapes, strict=True):
        n = piece.shape[0]
        rows_buf[done : done + n, :] = piece[...]
        done += n
    products = lax.dot_general(
        proj_ref[...], rows_buf[...], contract_last, preferred_element_type=jnp.float32
    )
    for b, at in enumerate(sum(shapes, ())):
        here = slice(b * shard, (b + 1) * shard)
        top, share, prec, may = (meta_row(at, row) for row in range(4))
        mine = prec * (products[:, here] - half_ref[...])
        for t in range(tiles_here):
            down = slice(t * tile, (t + 1) * tile)
            mark = jnp.where(lane == chip * tiles_here + t, may, 0.0)
            floor = jnp.where(jnp.max(mark, axis=1, keepdims=True) > 0, -top, very_low)
            weights_buf[down, here] = (jnp.exp(mine[down, :] + floor) * share).astype(
                jnp.bfloat16
            )
        seen += weights_buf[:, here].astype(jnp.float32)
    if not first:
        seen += cnt_ref[...]
    if last:
        kept_ref, kept_cnt_ref, sent_ref = outs
        half_width = width // 2
        keep = pl.ds(pl.multiple_of(core * half_width, half_width), half_width)
        send = pl.ds(pl.multiple_of((1 - core) * half_width, half_width), half_width)
        seen_buf[...] = jnp.broadcast_to(jnp.sum(seen, axis=1, keepdims=True), seen.shape)
        kept_cnt_ref[...] = seen_buf[keep, :]
        sent_ref[:, columns:] = seen_buf[send, :].astype(jnp.bfloat16)
        targets = ((send, sent_ref), (keep, kept_ref))
    else:
        outs[1][...] = seen
        targets = ((pl.ds(0, width), outs[0]),)
    chunk = min(columns, 512)
    for where, out in targets:
        for c in range(0, columns, chunk):
            part = slice(c, c + chunk)
            sums = lax.dot_general(
                weights_buf[where, :],
                rows_buf[:, part],
                (((1,), (0,)), ((), ())),
                preferred_element_type=jnp.float32,
            )
            if not first:
                sums += acc_ref[where, part]
            out[:, part] = sums.astype(out.dtype)


def final_kernel(kept_ref, kept_cnt_ref, got_ref, proj_ref, out_ref):
    rows, columns = out_ref.shape
    core = lax.rem(lax.axis_index("img"), cores)
    here = pl.ds(pl.multiple_of(pl.program_id(0) * rows, rows), rows)
    first_row = (core * pl.num_programs(0) + pl.program_id(0)) * rows
    counts = kept_cnt_ref[here, 0:1] + got_ref[here, columns : columns + 1].astype(jnp.float32)
    sums = kept_ref[here, :] + got_ref[here, :columns].astype(jnp.float32)
    prior = prior_weight * proj_ref[pl.ds(pl.multiple_of(first_row, rows), rows), :].astype(
        jnp.float32
    )
    out_ref[...] = (sums + prior) * (1.0 / (counts + prior_weight))


def gathered_body(n_img, n_ori, images, precision, projections, tile_mask):
    n = n_img * n_ori
    shard, columns = images.shape
    orient = projections.shape[0]
    chips = n_img // cores
    width = orient // chips
    blocks, tiles = tile_mask.shape
    f32 = jnp.float32
    limit = pltpu.CompilerParams(vmem_limit_bytes=14 * 2**20)

    def swap(a, even, odd=None):
        masks = [d[0] * cores * n_ori + d[1] for d in (even, odd or even)]
        return lax.ppermute(a, both, [(i, i ^ masks[i // n_ori % cores]) for i in range(n)])

    def moved(shards, even, odd=None):
        odd = odd or even
        return tuple(
            ((e[0] ^ even[0], e[1] ^ even[1]), (o[0] ^ odd[0], o[1] ^ odd[1])) for e, o in shards
        )

    x, y = (0, 1), (1, 0)
    near, far = (x, y), (y, x)

    def sent(piece, even, odd=None):
        return moved(piece[0], even, odd), swap(piece[1], even, odd)

    def together(values):
        leaves, tree = jax.tree.flatten(values)
        arrays = iter(lax.optimization_barrier([a for a in leaves if not isinstance(a, int)]))
        return tree.unflatten([a if isinstance(a, int) else next(arrays) for a in leaves])

    lowered = images.astype(jnp.bfloat16)
    own = ((((0, 0), (0, 0)),), lowered)
    near_slab, far_slab = sent(own, (2, 0)), sent(own, (4, 0))
    own_a, own_b = sent(own, *near), sent(own, *far)

    prec_row = precision.reshape(1, -1)
    rows = prec_row.shape[1]
    held, held_chip, half_row, half_col = pl.pallas_call(
        functools.partial(load_kernel, chips),
        in_specs=[pl.BlockSpec(memory_space=pltpu.HBM)],
        out_specs=[vmem] * 4,
        out_shape=[
            pltpu.VMEM(projections.shape, projections.dtype),
            jax.ShapeDtypeStruct((width, columns), projections.dtype),
            jax.ShapeDtypeStruct((8, orient), f32),
            jax.ShapeDtypeStruct((width, lanes), f32),
        ],
        scratch_shapes=[pltpu.SemaphoreType.DMA((chips + 1,))],
        compiler_params=limit,
        cost_estimate=pl.CostEstimate(flops=0, bytes_accessed=0, transcendentals=0),
        name="load",
    )(pltpu.with_memory_space_constraint(projections, pltpu.HBM))
    held = pltpu.with_memory_space_constraint(held, pltpu.VMEM)
    own_a, own_b, held_chip, half_row, half_col = together(
        (own_a, own_b, held_chip, half_row, half_col)
    )
    own_c = sent(own_a, *far)
    whole = lambda i: (0, 0)
    scores, stats = pl.pallas_call(
        functools.partial(scores_kernel, chips),
        in_specs=[smem] + [vmem] * 6,
        out_specs=[vmem] * 2,
        out_shape=[
            pltpu.VMEM((rows, orient), f32),
            jax.ShapeDtypeStruct((8, rows), f32),
        ],
        scratch_shapes=[pltpu.VMEM((rows, columns), jnp.bfloat16)],
        compiler_params=limit,
        cost_estimate=pl.CostEstimate(flops=0, bytes_accessed=0, transcendentals=0),
        name="scores",
    )(tile_mask, prec_row, half_row, lowered, own_a[1], own_b[1], held)
    theirs = swap(stats, x)
    meta = pl.pallas_call(
        meta_kernel,
        in_specs=[smem, vmem, vmem, vmem],
        out_specs=vmem,
        out_shape=jax.ShapeDtypeStruct((n_ori, 8, shard), f32),
        compiler_params=limit,
        cost_estimate=pl.CostEstimate(flops=0, bytes_accessed=0, transcendentals=0),
        name="meta",
    )(tile_mask, prec_row, stats, theirs)
    from_y = swap(meta, y)
    far_slab, near_slab, own_c, meta, scores = together(
        (far_slab, near_slab, own_c, meta, scores)
    )
    last_slab = sent(far_slab, (2, 0))
    far_a, far_b = sent(far_slab, *near), sent(far_slab, *far)
    cut = 4
    posteriors = pl.pallas_call(
        posterior_kernel,
        grid=(cut,),
        in_specs=[
            vmem,
            pl.BlockSpec((8, rows), whole),
            pl.BlockSpec((8, rows), whole),
        ],
        out_specs=pl.BlockSpec((rows, orient // cut), lambda i: (0, i)),
        out_shape=jax.ShapeDtypeStruct((rows, orient), jnp.bfloat16),
        compiler_params=limit,
        cost_estimate=pl.CostEstimate(flops=0, bytes_accessed=0, transcendentals=0),
        name="posterior",
    )(scores, stats, theirs)

    far_a, far_b, last_slab, from_y, meta, posteriors = together(
        (far_a, far_b, last_slab, from_y, meta, posteriors)
    )
    far_c = sent(far_a, *far)
    last_a, last_b = sent(last_slab, *near), sent(last_slab, *far)
    metas = jnp.concatenate([meta, from_y], axis=0)
    metas = jnp.concatenate([metas, swap(metas, (2, 0))], axis=0)
    metas = [metas, swap(metas, (4, 0))]
    metas, own_b, own_c = together((metas, own_b, own_c))
    half_shard = shard // 2
    near_b = moved(own_b[0], (2, 0)), swap(own_b[1][:half_shard], (2, 0))
    near_c = sent(own_c, (2, 0))

    def add(group, state, last):
        shapes = tuple(shards for shards, _ in group)
        pieces = [a for _, a in group]
        images_here = sum(a.shape[0] for a in pieces)
        first = state is None
        if last:
            out_shape = [
                jax.ShapeDtypeStruct((width // 2, columns), f32),
                jax.ShapeDtypeStruct((width // 2, lanes), f32),
                jax.ShapeDtypeStruct((width // 2, columns + lanes), jnp.bfloat16),
            ]
        else:
            out_shape = [
                jax.ShapeDtypeStruct((width, columns), f32),
                jax.ShapeDtypeStruct((width, lanes), f32),
            ]
        n_ins = 2 + len(metas) + len(pieces) + (0 if first else 2)
        return pl.pallas_call(
            functools.partial(sums_kernel, len(metas), tiles * cores // n_img, shapes, first, last),
            in_specs=[vmem] * n_ins,
            out_specs=[vmem] * len(out_shape),
            out_shape=out_shape,
            input_output_aliases={} if first or last else {n_ins - 2: 0, n_ins - 1: 1},
            scratch_shapes=[
                pltpu.VMEM((images_here, columns), jnp.bfloat16),
                pltpu.VMEM((width, images_here), jnp.bfloat16),
                pltpu.VMEM((width, lanes), f32),
            ],
            compiler_params=limit,
        cost_estimate=pl.CostEstimate(flops=0, bytes_accessed=0, transcendentals=0),
            name="sums",
        )(half_col, held_chip, *metas, *pieces, *(state or ()))

    state = add([own, own_a, own_b, own_c], None, False)
    state = add([near_slab, far_slab, far_a, far_b], state, False)
    state, near_slab, far_c, last_a = together((state, near_slab, far_c, last_a))
    last_c = sent(last_a, *far)
    near_a = sent(near_slab, *near)
    near_b_low = (), swap(near_slab[1][half_shard:], *far)
    state, last_b = together((state, last_b))
    state = add([far_c, last_slab, last_a, last_b], state, False)
    kept, kept_cnt, sent_away = add([near_a, near_b, near_b_low, near_c, last_c], state, True)
    got = lax.ppermute(sent_away, both, [(i, i ^ n_ori) for i in range(n)])
    out_rows = width // 2
    cut = 4
    refined = pl.pallas_call(
        final_kernel,
        grid=(cut,),
        in_specs=[vmem] * 4,
        out_specs=pl.BlockSpec((out_rows // cut, columns), lambda i: (i, 0)),
        out_shape=jax.ShapeDtypeStruct((out_rows, columns), f32),
        compiler_params=limit,
        cost_estimate=pl.CostEstimate(flops=0, bytes_accessed=0, transcendentals=0),
        name="final",
    )(kept, kept_cnt, got, held_chip)
    return posteriors, refined


def solution(mesh):
    n_img, n_ori = mesh.shape["img"], mesh.shape["ori"]

    def body(images, precision, projections, tile_mask):
        shard, columns = images.shape
        orient = projections.shape[0]
        blocks, tiles = tile_mask.shape
        gathered_bytes = 2 * images.size * n_img * n_ori // cores
        fits = (
            n_ori == 2
            and n_img == 8 * cores
            and blocks == n_ori
            and shard % lanes == 0
            and tiles * cores % n_img == 0
            and orient % (tiles * lanes) == 0
            and tiles <= shard
            and gathered_bytes <= 16 * 2**20
        )
        if fits:
            return gathered_body(n_img, n_ori, images, precision, projections, tile_mask)
        return reduced_body(images, precision, projections, tile_mask)

    return jax.shard_map(
        body,
        mesh=mesh,
        in_specs=(P(("img", "ori"), None), P("img"), P("ori", None), P("img", "ori")),
        out_specs=(P("img", "ori"), P(("ori", "img"), None)),
        check_vma=False,
    )
```

```python
import functools

import jax
import jax.numpy as jnp
from jax import lax
from jax.experimental import pallas as pl
from jax.experimental.pallas import tpu as pltpu
from jax.sharding import PartitionSpec as P

prior_weight = 1.0
very_low = -1e30
both = ("img", "ori")
lanes = 128
cores = 2
vmem = pl.BlockSpec(memory_space=pltpu.VMEM)
smem = pl.BlockSpec(memory_space=pltpu.SMEM)
contract_last = (((1,), (1,)), ((), ()))


def weighted_sums(weights, rows_block):
    return lax.dot_general(
        weights, rows_block, (((0,), (0,)), ((), ())), preferred_element_type=jnp.float32
    )


def reduced_body(images, precision, projections, tile_mask):
    lowered = images.astype(jnp.bfloat16)
    grouped = lax.all_gather(lowered, "ori", axis=0, tiled=True)
    proj_float = projections.astype(jnp.float32)
    squared = jnp.sum(proj_float * proj_float, axis=1)
    blocks, tiles_here = tile_mask.shape
    per_block = grouped.shape[0] // blocks
    tile_width = projections.shape[0] // tiles_here
    columns = grouped.shape[1]
    products = lax.dot_general(
        grouped, projections, contract_last, preferred_element_type=jnp.float32
    )
    scores = precision[:, None] * (products - 0.5 * squared[None, :])
    shaped = scores.reshape(blocks, per_block, tiles_here, tile_width)
    alive = jnp.broadcast_to((tile_mask > 0)[:, None, :, None], shaped.shape)
    masked = jnp.where(alive, shaped, very_low)
    local_high = jnp.max(masked, axis=(2, 3))
    row_high = lax.pmax(local_high, "ori")
    lifted = jnp.where(alive, jnp.exp(masked - row_high[:, :, None, None]), 0.0)
    row_total = lax.psum(jnp.sum(lifted, axis=(2, 3)), "ori")
    probable = lifted / row_total[:, :, None, None]
    posteriors = probable.reshape(scores.shape).astype(jnp.bfloat16)
    counts = jnp.sum(posteriors.astype(jnp.float32), axis=0)
    half_width = columns // 2
    halves = [
        lax.psum_scatter(
            weighted_sums(posteriors, part).astype(jnp.bfloat16),
            "img",
            scatter_dimension=0,
            tiled=True,
        ).astype(jnp.float32)
        for part in (grouped[:, :half_width], grouped[:, half_width:])
    ]
    totals = lax.psum_scatter(
        counts.astype(jnp.bfloat16), "img", scatter_dimension=0, tiled=True
    ).astype(jnp.float32)
    summed = jnp.concatenate(halves, axis=1)
    rows_here = summed.shape[0]
    first_row = lax.axis_index("img") * rows_here
    prior_rows = lax.dynamic_slice_in_dim(proj_float, first_row, rows_here, 0)
    refined = (summed + prior_weight * prior_rows) / (totals[:, None] + prior_weight)
    return (posteriors, refined)


def as_row(column):
    return jnp.transpose(jnp.broadcast_to(column, (column.shape[0], lanes)))[0:1, :]


def as_column(row):
    return jnp.transpose(jnp.broadcast_to(row, (lanes, row.shape[1])))[:, 0:1]


def load_kernel(chips, away_ref, proj_ref, mine_ref, row_ref, col_ref, sems):
    width = proj_ref.shape[0] // chips
    chip = lax.axis_index("img") // cores

    def copy(i):
        rows = pl.ds(pl.multiple_of(i * width, width), width)
        return pltpu.make_async_copy(away_ref.at[rows], proj_ref.at[rows], sems.at[i])

    for i in range(chips):
        copy(i).start()
    mine = pltpu.make_async_copy(
        away_ref.at[pl.ds(pl.multiple_of(chip * width, width), width)], mine_ref, sems.at[chips]
    )
    mine.start()

    @pl.loop(0, chips)
    def _(i):
        copy(i).wait()
        here = pl.ds(pl.multiple_of(i * width, width), width)
        wide = proj_ref[here, :].astype(jnp.float32)
        half = 0.5 * jnp.sum(wide * wide, axis=1, keepdims=True)
        half_wide = jnp.broadcast_to(half, (width, lanes))
        row_ref[:, here] = jnp.transpose(half_wide)[0:8, :]

        @pl.when(i == chip)
        def _():
            col_ref[...] = half_wide

    mine.wait()


def scores_kernel(
    chips, mask_s, prec_ref, half_ref, own_ref, first_ref, second_ref, proj_ref, scores_ref, stats_ref,
    rows_buf,
):
    here = lax.axis_index("ori")
    core = lax.rem(lax.axis_index("img"), cores)
    shard = own_ref.shape[0]
    blocks, tiles = mask_s.shape
    width = proj_ref.shape[0] // chips
    tiles_here = tiles // chips
    tile = width // tiles_here
    rows_buf[pl.ds(pl.multiple_of(here * shard, shard), shard), :] = own_ref[...]
    there = pl.ds(pl.multiple_of((1 - here) * shard, shard), shard)

    @pl.when(core == 0)
    def _():
        rows_buf[there, :] = first_ref[...]

    @pl.when(core != 0)
    def _():
        rows_buf[there, :] = second_ref[...]

    prec_col = as_column(prec_ref[...])
    high = [jnp.full((shard, lanes), very_low, jnp.float32)] * blocks
    total = [jnp.zeros((shard, lanes), jnp.float32)] * blocks
    for step in range(chips):
        where = slice(step * width, (step + 1) * width)
        products = lax.dot_general(
            rows_buf[...], proj_ref[where, :], contract_last, preferred_element_type=jnp.float32
        )
        scores = prec_col * (products - half_ref[0:1, where])
        for b in range(blocks):
            rows = slice(b * shard, (b + 1) * shard)
            parts = []
            for t in range(tiles_here):
                at = step * width + t * tile
                alive = mask_s[b, step * tiles_here + t] > 0
                kept = jnp.where(alive, scores[rows, t * tile : (t + 1) * tile], very_low)
                scores_ref[rows, at : at + tile] = kept
                parts += [kept[:, c : c + lanes] for c in range(0, tile, lanes)]
            now = functools.reduce(jnp.maximum, parts, high[b])
            added = functools.reduce(jnp.add, [jnp.exp(part - now) for part in parts])
            total[b] = total[b] * jnp.exp(high[b] - now) + added
            high[b] = now
    for b in range(blocks):
        rows = slice(b * shard, (b + 1) * shard)
        top = jnp.max(high[b], axis=1, keepdims=True)
        mass = jnp.sum(total[b] * jnp.exp(high[b] - top), axis=1, keepdims=True)
        stats_ref[0:1, rows] = as_row(top)
        stats_ref[1:2, rows] = as_row(mass)
    stats_ref[2:8, :] = jnp.zeros((6, stats_ref.shape[1]), jnp.float32)


def joined(mine_ref, theirs_ref):
    top = jnp.maximum(mine_ref[0:1, :], theirs_ref[0:1, :])
    mass = mine_ref[1:2, :] * jnp.exp(mine_ref[0:1, :] - top) + theirs_ref[
        1:2, :
    ] * jnp.exp(theirs_ref[0:1, :] - top)
    return top, 1.0 / mass


def meta_kernel(mask_s, prec_ref, mine_ref, theirs_ref, meta_ref):
    top, share = joined(mine_ref, theirs_ref)
    parts, _, shard = meta_ref.shape
    tiles = mask_s.shape[1]
    at = lax.broadcasted_iota(jnp.int32, (1, shard), 1)
    for b in range(parts):
        columns = slice(b * shard, (b + 1) * shard)
        meta_ref[b, 0:1, :] = top[:, columns]
        meta_ref[b, 1:2, :] = share[:, columns]
        meta_ref[b, 2:3, :] = prec_ref[:, columns]
        may = jnp.zeros((1, shard), jnp.float32)
        for t in range(tiles):
            may = jnp.where((at == t) & (mask_s[b, t] > 0), 1.0, may)
        meta_ref[b, 3:4, :] = may
        meta_ref[b, 4:8, :] = jnp.zeros((4, shard), jnp.float32)


def posterior_kernel(scores_ref, mine_ref, theirs_ref, post_ref):
    top, share = joined(mine_ref, theirs_ref)
    n = post_ref.shape[1]
    here = pl.ds(pl.multiple_of(pl.program_id(0) * n, n), n)
    post_ref[...] = (
        jnp.exp(scores_ref[:, here] - as_column(top)) * as_column(share)
    ).astype(post_ref.dtype)


def sums_kernel(n_metas, tiles_here, shapes, first, last, *refs):
    half_ref, proj_ref = refs[:2]
    metas, refs = refs[2 : 2 + n_metas], refs[2 + n_metas :]
    pieces, refs = refs[: len(shapes)], refs[len(shapes) :]
    if not first:
        acc_ref, cnt_ref = refs[:2]
        refs = refs[2:]
    n_outs = 3 if last else 2
    outs, (rows_buf, weights_buf, seen_buf) = refs[:n_outs], refs[n_outs:]
    img, ori = lax.axis_index("img"), lax.axis_index("ori")
    chip, core = img // cores, lax.rem(img, cores)
    width, columns = proj_ref.shape
    n_ori = lax.axis_size("ori")
    per_meta, _, shard = metas[0].shape
    tile = width // tiles_here
    seen = jnp.zeros((width, shard), jnp.float32)
    lane = lax.broadcasted_iota(jnp.int32, (1, shard), 1)

    def meta_row(at, row):
        def read(d):
            which, inner = divmod(d[0] * n_ori, per_meta)
            return metas[which][inner + (ori ^ d[1]), pl.ds(row, 1), :]

        if at[0] == at[1]:
            return read(at[0])
        return jnp.where(core == 0, read(at[0]), read(at[1]))

    done = 0
    for piece, shards in zip(pieces, shapes, strict=True):
        n = piece.shape[0]
        rows_buf[done : done + n, :] = piece[...]
        done += n
    products = lax.dot_general(
        proj_ref[...], rows_buf[...], contract_last, preferred_element_type=jnp.float32
    )
    for b, at in enumerate(sum(shapes, ())):
        here = slice(b * shard, (b + 1) * shard)
        top, share, prec, may = (meta_row(at, row) for row in range(4))
        mine = prec * (products[:, here] - half_ref[...])
        for t in range(tiles_here):
            down = slice(t * tile, (t + 1) * tile)
            mark = jnp.where(lane == chip * tiles_here + t, may, 0.0)
            floor = jnp.where(jnp.max(mark, axis=1, keepdims=True) > 0, -top, very_low)
            weights_buf[down, here] = (jnp.exp(mine[down, :] + floor) * share).astype(
                jnp.bfloat16
            )
        seen += weights_buf[:, here].astype(jnp.float32)
    if not first:
        seen += cnt_ref[...]
    if last:
        kept_weights_ref, kept_cnt_ref, sent_ref = outs
        half_width = width // 2
        keep = pl.ds(pl.multiple_of(core * half_width, half_width), half_width)
        send = pl.ds(pl.multiple_of((1 - core) * half_width, half_width), half_width)
        seen_buf[...] = jnp.broadcast_to(jnp.sum(seen, axis=1, keepdims=True), seen.shape)
        kept_cnt_ref[...] = seen_buf[keep, :]
        sent_ref[:, columns:] = seen_buf[send, :].astype(jnp.bfloat16)
        kept_weights_ref[...] = weights_buf[keep, :]
        targets = ((send, sent_ref),)
    else:
        outs[1][...] = seen
        targets = ((pl.ds(0, width), outs[0]),)
    chunk = min(columns, 512)
    for where, out in targets:
        for c in range(0, columns, chunk):
            part = slice(c, c + chunk)
            sums = lax.dot_general(
                weights_buf[where, :],
                rows_buf[:, part],
                (((1,), (0,)), ((), ())),
                preferred_element_type=jnp.float32,
            )
            if not first:
                sums += acc_ref[where, part]
            out[:, part] = sums.astype(out.dtype)


def keep_kernel(acc_ref, weights_ref, *refs):
    pieces, (kept_ref, rows_buf) = refs[:-2], refs[-2:]
    done = 0
    for piece in pieces:
        n = piece.shape[0]
        rows_buf[done : done + n, :] = piece[...]
        done += n
    rows, columns = kept_ref.shape
    core = lax.rem(lax.axis_index("img"), cores)
    keep = pl.ds(pl.multiple_of(core * rows, rows), rows)
    chunk = min(columns, 512)
    for c in range(0, columns, chunk):
        part = slice(c, c + chunk)
        kept_ref[:, part] = acc_ref[keep, part] + lax.dot_general(
            weights_ref[...],
            rows_buf[:, part],
            (((1,), (0,)), ((), ())),
            preferred_element_type=jnp.float32,
        )


def final_kernel(kept_ref, kept_cnt_ref, got_ref, proj_ref, out_ref):
    rows, columns = out_ref.shape
    core = lax.rem(lax.axis_index("img"), cores)
    here = pl.ds(pl.multiple_of(pl.program_id(0) * rows, rows), rows)
    first_row = (core * pl.num_programs(0) + pl.program_id(0)) * rows
    counts = kept_cnt_ref[here, 0:1] + got_ref[here, columns : columns + 1].astype(jnp.float32)
    sums = kept_ref[here, :] + got_ref[here, :columns].astype(jnp.float32)
    prior = prior_weight * proj_ref[pl.ds(pl.multiple_of(first_row, rows), rows), :].astype(
        jnp.float32
    )
    out_ref[...] = (sums + prior) * (1.0 / (counts + prior_weight))


def gathered_body(n_img, n_ori, images, precision, projections, tile_mask):
    n = n_img * n_ori
    shard, columns = images.shape
    orient = projections.shape[0]
    chips = n_img // cores
    width = orient // chips
    blocks, tiles = tile_mask.shape
    f32 = jnp.float32
    limit = pltpu.CompilerParams(vmem_limit_bytes=14 * 2**20)

    def swap(a, even, odd=None):
        masks = [d[0] * cores * n_ori + d[1] for d in (even, odd or even)]
        return lax.ppermute(a, both, [(i, i ^ masks[i // n_ori % cores]) for i in range(n)])

    def moved(shards, even, odd=None):
        odd = odd or even
        return tuple(
            ((e[0] ^ even[0], e[1] ^ even[1]), (o[0] ^ odd[0], o[1] ^ odd[1])) for e, o in shards
        )

    x, y = (0, 1), (1, 0)
    near, far = (x, y), (y, x)

    def sent(piece, even, odd=None):
        return moved(piece[0], even, odd), swap(piece[1], even, odd)

    def together(values):
        leaves, tree = jax.tree.flatten(values)
        arrays = iter(lax.optimization_barrier([a for a in leaves if not isinstance(a, int)]))
        return tree.unflatten([a if isinstance(a, int) else next(arrays) for a in leaves])

    lowered = images.astype(jnp.bfloat16)
    own = ((((0, 0), (0, 0)),), lowered)
    near_slab, far_slab = sent(own, (2, 0)), sent(own, (4, 0))
    own_a, own_b = sent(own, *near), sent(own, *far)

    prec_row = precision.reshape(1, -1)
    rows = prec_row.shape[1]
    held, held_chip, half_row, half_col = pl.pallas_call(
        functools.partial(load_kernel, chips),
        in_specs=[pl.BlockSpec(memory_space=pltpu.HBM)],
        out_specs=[vmem] * 4,
        out_shape=[
            pltpu.VMEM(projections.shape, projections.dtype),
            jax.ShapeDtypeStruct((width, columns), projections.dtype),
            jax.ShapeDtypeStruct((8, orient), f32),
            jax.ShapeDtypeStruct((width, lanes), f32),
        ],
        scratch_shapes=[pltpu.SemaphoreType.DMA((chips + 1,))],
        compiler_params=limit,
        cost_estimate=pl.CostEstimate(flops=0, bytes_accessed=0, transcendentals=0),
        name="load",
    )(pltpu.with_memory_space_constraint(projections, pltpu.HBM))
    held = pltpu.with_memory_space_constraint(held, pltpu.VMEM)
    own_a, own_b, held_chip, half_row, half_col = together(
        (own_a, own_b, held_chip, half_row, half_col)
    )
    own_c = sent(own_a, *far)
    whole = lambda i: (0, 0)
    scores, stats = pl.pallas_call(
        functools.partial(scores_kernel, chips),
        in_specs=[smem] + [vmem] * 6,
        out_specs=[vmem] * 2,
        out_shape=[
            pltpu.VMEM((rows, orient), f32),
            jax.ShapeDtypeStruct((8, rows), f32),
        ],
        scratch_shapes=[pltpu.VMEM((rows, columns), jnp.bfloat16)],
        compiler_params=limit,
        cost_estimate=pl.CostEstimate(flops=0, bytes_accessed=0, transcendentals=0),
        name="scores",
    )(tile_mask, prec_row, half_row, lowered, own_a[1], own_b[1], held)
    theirs = swap(stats, x)
    meta = pl.pallas_call(
        meta_kernel,
        in_specs=[smem, vmem, vmem, vmem],
        out_specs=vmem,
        out_shape=jax.ShapeDtypeStruct((n_ori, 8, shard), f32),
        compiler_params=limit,
        cost_estimate=pl.CostEstimate(flops=0, bytes_accessed=0, transcendentals=0),
        name="meta",
    )(tile_mask, prec_row, stats, theirs)
    from_y = swap(meta, y)
    far_slab, near_slab, own_c, meta, scores = together(
        (far_slab, near_slab, own_c, meta, scores)
    )
    last_slab = sent(far_slab, (2, 0))
    far_a, far_b = sent(far_slab, *near), sent(far_slab, *far)
    cut = 4
    posteriors = pl.pallas_call(
        posterior_kernel,
        grid=(cut,),
        in_specs=[
            vmem,
            pl.BlockSpec((8, rows), whole),
            pl.BlockSpec((8, rows), whole),
        ],
        out_specs=pl.BlockSpec((rows, orient // cut), lambda i: (0, i)),
        out_shape=jax.ShapeDtypeStruct((rows, orient), jnp.bfloat16),
        compiler_params=limit,
        cost_estimate=pl.CostEstimate(flops=0, bytes_accessed=0, transcendentals=0),
        name="posterior",
    )(scores, stats, theirs)

    far_a, far_b, last_slab, from_y, meta, posteriors = together(
        (far_a, far_b, last_slab, from_y, meta, posteriors)
    )
    far_c = sent(far_a, *far)
    last_a, last_b = sent(last_slab, *near), sent(last_slab, *far)
    metas = jnp.concatenate([meta, from_y], axis=0)
    metas = jnp.concatenate([metas, swap(metas, (2, 0))], axis=0)
    metas = [metas, swap(metas, (4, 0))]
    metas, own_b, own_c = together((metas, own_b, own_c))
    by_z = shard // 4 * 3
    near_b = moved(own_b[0], (2, 0)), swap(own_b[1][:by_z], (2, 0))
    near_c = sent(own_c, (2, 0))

    def add(group, state, last):
        shapes = tuple(shards for shards, _ in group)
        pieces = [a for _, a in group]
        images_here = sum(a.shape[0] for a in pieces)
        first = state is None
        if last:
            out_shape = [
                jax.ShapeDtypeStruct((width // 2, images_here), jnp.bfloat16),
                jax.ShapeDtypeStruct((width // 2, lanes), f32),
                jax.ShapeDtypeStruct((width // 2, columns + lanes), jnp.bfloat16),
            ]
        else:
            out_shape = [
                jax.ShapeDtypeStruct((width, columns), f32),
                jax.ShapeDtypeStruct((width, lanes), f32),
            ]
        n_ins = 2 + len(metas) + len(pieces) + (0 if first else 2)
        return pl.pallas_call(
            functools.partial(sums_kernel, len(metas), tiles * cores // n_img, shapes, first, last),
            in_specs=[vmem] * n_ins,
            out_specs=[vmem] * len(out_shape),
            out_shape=out_shape,
            input_output_aliases={} if first or last else {n_ins - 2: 0, n_ins - 1: 1},
            scratch_shapes=[
                pltpu.VMEM((images_here, columns), jnp.bfloat16),
                pltpu.VMEM((width, images_here), jnp.bfloat16),
                pltpu.VMEM((width, lanes), f32),
            ],
            compiler_params=limit,
        cost_estimate=pl.CostEstimate(flops=0, bytes_accessed=0, transcendentals=0),
            name="sums",
        )(half_col, held_chip, *metas, *pieces, *(state or ()))

    state = add([own, own_a, own_b, own_c], None, False)
    state = add([near_slab, far_slab, far_a, far_b], state, False)
    state, near_slab, far_c, last_a = together((state, near_slab, far_c, last_a))
    last_c = sent(last_a, *far)
    near_a = sent(near_slab, *near)
    near_b_low = (), swap(near_slab[1][by_z:], *far)
    state, last_b = together((state, last_b))
    state = add([far_c, last_slab, last_a, last_b], state, False)
    final_group = [near_a, near_b, near_b_low, near_c, last_c]
    kept_weights, kept_cnt, sent_away = add(final_group, state, True)
    got = lax.ppermute(sent_away, both, [(i, i ^ n_ori) for i in range(n)])
    last_pieces = [a for _, a in final_group]
    kept = pl.pallas_call(
        keep_kernel,
        in_specs=[vmem] * (2 + len(last_pieces)),
        out_specs=vmem,
        out_shape=jax.ShapeDtypeStruct((width // 2, columns), f32),
        scratch_shapes=[pltpu.VMEM((kept_weights.shape[1], columns), jnp.bfloat16)],
        compiler_params=limit,
        cost_estimate=pl.CostEstimate(flops=0, bytes_accessed=0, transcendentals=0),
        name="keep",
    )(state[0], kept_weights, *last_pieces)
    out_rows = width // 2
    cut = 4
    refined = pl.pallas_call(
        final_kernel,
        grid=(cut,),
        in_specs=[vmem] * 4,
        out_specs=pl.BlockSpec((out_rows // cut, columns), lambda i: (i, 0)),
        out_shape=jax.ShapeDtypeStruct((out_rows, columns), f32),
        compiler_params=limit,
        cost_estimate=pl.CostEstimate(flops=0, bytes_accessed=0, transcendentals=0),
        name="final",
    )(kept, kept_cnt, got, held_chip)
    return posteriors, refined


def solution(mesh):
    n_img, n_ori = mesh.shape["img"], mesh.shape["ori"]

    def body(images, precision, projections, tile_mask):
        shard, columns = images.shape
        orient = projections.shape[0]
        blocks, tiles = tile_mask.shape
        gathered_bytes = 2 * images.size * n_img * n_ori // cores
        fits = (
            n_ori == 2
            and n_img == 8 * cores
            and blocks == n_ori
            and shard % lanes == 0
            and tiles * cores % n_img == 0
            and orient % (tiles * lanes) == 0
            and tiles <= shard
            and gathered_bytes <= 16 * 2**20
        )
        if fits:
            return gathered_body(n_img, n_ori, images, precision, projections, tile_mask)
        return reduced_body(images, precision, projections, tile_mask)

    return jax.shard_map(
        body,
        mesh=mesh,
        in_specs=(P(("img", "ori"), None), P("img"), P("ori", None), P("img", "ori")),
        out_specs=(P("img", "ori"), P(("ori", "img"), None)),
        check_vma=False,
    )
```

```python
import functools

import jax
import jax.numpy as jnp
from jax import lax
from jax.experimental import pallas as pl
from jax.experimental.pallas import tpu as pltpu
from jax.sharding import PartitionSpec as P

prior_weight = 1.0
very_low = -1e30
both = ("img", "ori")
lanes = 128
cores = 2
vmem = pl.BlockSpec(memory_space=pltpu.VMEM)
smem = pl.BlockSpec(memory_space=pltpu.SMEM)
contract_last = (((1,), (1,)), ((), ()))


def weighted_sums(weights, rows_block):
    return lax.dot_general(
        weights, rows_block, (((0,), (0,)), ((), ())), preferred_element_type=jnp.float32
    )


def reduced_body(images, precision, projections, tile_mask):
    lowered = images.astype(jnp.bfloat16)
    grouped = lax.all_gather(lowered, "ori", axis=0, tiled=True)
    proj_float = projections.astype(jnp.float32)
    squared = jnp.sum(proj_float * proj_float, axis=1)
    blocks, tiles_here = tile_mask.shape
    per_block = grouped.shape[0] // blocks
    tile_width = projections.shape[0] // tiles_here
    columns = grouped.shape[1]
    products = lax.dot_general(
        grouped, projections, contract_last, preferred_element_type=jnp.float32
    )
    scores = precision[:, None] * (products - 0.5 * squared[None, :])
    shaped = scores.reshape(blocks, per_block, tiles_here, tile_width)
    alive = jnp.broadcast_to((tile_mask > 0)[:, None, :, None], shaped.shape)
    masked = jnp.where(alive, shaped, very_low)
    local_high = jnp.max(masked, axis=(2, 3))
    row_high = lax.pmax(local_high, "ori")
    lifted = jnp.where(alive, jnp.exp(masked - row_high[:, :, None, None]), 0.0)
    row_total = lax.psum(jnp.sum(lifted, axis=(2, 3)), "ori")
    probable = lifted / row_total[:, :, None, None]
    posteriors = probable.reshape(scores.shape).astype(jnp.bfloat16)
    counts = jnp.sum(posteriors.astype(jnp.float32), axis=0)
    half_width = columns // 2
    halves = [
        lax.psum_scatter(
            weighted_sums(posteriors, part).astype(jnp.bfloat16),
            "img",
            scatter_dimension=0,
            tiled=True,
        ).astype(jnp.float32)
        for part in (grouped[:, :half_width], grouped[:, half_width:])
    ]
    totals = lax.psum_scatter(
        counts.astype(jnp.bfloat16), "img", scatter_dimension=0, tiled=True
    ).astype(jnp.float32)
    summed = jnp.concatenate(halves, axis=1)
    rows_here = summed.shape[0]
    first_row = lax.axis_index("img") * rows_here
    prior_rows = lax.dynamic_slice_in_dim(proj_float, first_row, rows_here, 0)
    refined = (summed + prior_weight * prior_rows) / (totals[:, None] + prior_weight)
    return (posteriors, refined)


def as_row(column):
    return jnp.transpose(jnp.broadcast_to(column, (column.shape[0], lanes)))[0:1, :]


def as_column(row):
    return jnp.transpose(jnp.broadcast_to(row, (lanes, row.shape[1])))[:, 0:1]


def load_kernel(chips, away_ref, proj_ref, mine_ref, row_ref, col_ref, sems):
    width = proj_ref.shape[0] // chips
    chip = lax.axis_index("img") // cores

    def copy(i):
        rows = pl.ds(pl.multiple_of(i * width, width), width)
        return pltpu.make_async_copy(away_ref.at[rows], proj_ref.at[rows], sems.at[i])

    for i in range(chips):
        copy(i).start()
    mine = pltpu.make_async_copy(
        away_ref.at[pl.ds(pl.multiple_of(chip * width, width), width)], mine_ref, sems.at[chips]
    )
    mine.start()

    @pl.loop(0, chips)
    def _(i):
        copy(i).wait()
        here = pl.ds(pl.multiple_of(i * width, width), width)
        wide = proj_ref[here, :].astype(jnp.float32)
        half = 0.5 * jnp.sum(wide * wide, axis=1, keepdims=True)
        half_wide = jnp.broadcast_to(half, (width, lanes))
        row_ref[:, here] = jnp.transpose(half_wide)[0:8, :]

        @pl.when(i == chip)
        def _():
            col_ref[...] = half_wide

    mine.wait()


def scores_kernel(
    chips, mask_s, prec_ref, half_ref, own_ref, first_ref, second_ref, proj_ref, scores_ref, stats_ref,
    rows_buf,
):
    here = lax.axis_index("ori")
    core = lax.rem(lax.axis_index("img"), cores)
    shard = own_ref.shape[0]
    blocks, tiles = mask_s.shape
    width = proj_ref.shape[0] // chips
    tiles_here = tiles // chips
    tile = width // tiles_here
    rows_buf[pl.ds(pl.multiple_of(here * shard, shard), shard), :] = own_ref[...]
    there = pl.ds(pl.multiple_of((1 - here) * shard, shard), shard)

    @pl.when(core == 0)
    def _():
        rows_buf[there, :] = first_ref[...]

    @pl.when(core != 0)
    def _():
        rows_buf[there, :] = second_ref[...]

    prec_col = as_column(prec_ref[...])
    high = [jnp.full((shard, lanes), very_low, jnp.float32)] * blocks
    total = [jnp.zeros((shard, lanes), jnp.float32)] * blocks
    for step in range(chips):
        where = slice(step * width, (step + 1) * width)
        products = lax.dot_general(
            rows_buf[...], proj_ref[where, :], contract_last, preferred_element_type=jnp.float32
        )
        scores = prec_col * (products - half_ref[0:1, where])
        for b in range(blocks):
            rows = slice(b * shard, (b + 1) * shard)
            parts = []
            for t in range(tiles_here):
                at = step * width + t * tile
                alive = mask_s[b, step * tiles_here + t] > 0
                kept = jnp.where(alive, scores[rows, t * tile : (t + 1) * tile], very_low)
                scores_ref[rows, at : at + tile] = kept
                parts += [kept[:, c : c + lanes] for c in range(0, tile, lanes)]
            now = functools.reduce(jnp.maximum, parts, high[b])
            added = functools.reduce(jnp.add, [jnp.exp(part - now) for part in parts])
            total[b] = total[b] * jnp.exp(high[b] - now) + added
            high[b] = now
    for b in range(blocks):
        rows = slice(b * shard, (b + 1) * shard)
        top = jnp.max(high[b], axis=1, keepdims=True)
        mass = jnp.sum(total[b] * jnp.exp(high[b] - top), axis=1, keepdims=True)
        stats_ref[0:1, rows] = as_row(top)
        stats_ref[1:2, rows] = as_row(mass)
    stats_ref[2:8, :] = jnp.zeros((6, stats_ref.shape[1]), jnp.float32)


def joined(mine_ref, theirs_ref):
    top = jnp.maximum(mine_ref[0:1, :], theirs_ref[0:1, :])
    mass = mine_ref[1:2, :] * jnp.exp(mine_ref[0:1, :] - top) + theirs_ref[
        1:2, :
    ] * jnp.exp(theirs_ref[0:1, :] - top)
    return top, 1.0 / mass


def meta_kernel(mask_s, prec_ref, mine_ref, theirs_ref, meta_ref):
    top, share = joined(mine_ref, theirs_ref)
    parts, _, shard = meta_ref.shape
    tiles = mask_s.shape[1]
    at = lax.broadcasted_iota(jnp.int32, (1, shard), 1)
    for b in range(parts):
        columns = slice(b * shard, (b + 1) * shard)
        meta_ref[b, 0:1, :] = top[:, columns]
        meta_ref[b, 1:2, :] = share[:, columns]
        meta_ref[b, 2:3, :] = prec_ref[:, columns]
        may = jnp.zeros((1, shard), jnp.float32)
        for t in range(tiles):
            may = jnp.where((at == t) & (mask_s[b, t] > 0), 1.0, may)
        meta_ref[b, 3:4, :] = may
        meta_ref[b, 4:8, :] = jnp.zeros((4, shard), jnp.float32)


def posterior_kernel(scores_ref, mine_ref, theirs_ref, post_ref):
    top, share = joined(mine_ref, theirs_ref)
    n = post_ref.shape[1]
    here = pl.ds(pl.multiple_of(pl.program_id(0) * n, n), n)
    post_ref[...] = (
        jnp.exp(scores_ref[:, here] - as_column(top)) * as_column(share)
    ).astype(post_ref.dtype)


def sums_kernel(n_metas, tiles_here, shapes, first, last, *refs):
    half_ref, proj_ref = refs[:2]
    metas, refs = refs[2 : 2 + n_metas], refs[2 + n_metas :]
    pieces, refs = refs[: len(shapes)], refs[len(shapes) :]
    if not first:
        acc_ref, cnt_ref = refs[:2]
        refs = refs[2:]
    n_outs = 3 if last else 2
    outs, (rows_buf, weights_buf, seen_buf) = refs[:n_outs], refs[n_outs:]
    img, ori = lax.axis_index("img"), lax.axis_index("ori")
    chip, core = img // cores, lax.rem(img, cores)
    width, columns = proj_ref.shape
    n_ori = lax.axis_size("ori")
    per_meta, _, shard = metas[0].shape
    tile = width // tiles_here
    seen = jnp.zeros((width, shard), jnp.float32)
    lane = lax.broadcasted_iota(jnp.int32, (1, shard), 1)

    def meta_row(at, row):
        def read(d):
            which, inner = divmod(d[0] * n_ori, per_meta)
            return metas[which][inner + (ori ^ d[1]), pl.ds(row, 1), :]

        if at[0] == at[1]:
            return read(at[0])
        return jnp.where(core == 0, read(at[0]), read(at[1]))

    done = 0
    for piece, shards in zip(pieces, shapes, strict=True):
        n = piece.shape[0]
        rows_buf[done : done + n, :] = piece[...]
        done += n
    products = lax.dot_general(
        proj_ref[...], rows_buf[...], contract_last, preferred_element_type=jnp.float32
    )
    for b, at in enumerate(sum(shapes, ())):
        here = slice(b * shard, (b + 1) * shard)
        top, share, prec, may = (meta_row(at, row) for row in range(4))
        mine = prec * (products[:, here] - half_ref[...])
        for t in range(tiles_here):
            down = slice(t * tile, (t + 1) * tile)
            mark = jnp.where(lane == chip * tiles_here + t, may, 0.0)
            floor = jnp.where(jnp.max(mark, axis=1, keepdims=True) > 0, -top, very_low)
            weights_buf[down, here] = (jnp.exp(mine[down, :] + floor) * share).astype(
                jnp.bfloat16
            )
        seen += weights_buf[:, here].astype(jnp.float32)
    if not first:
        seen += cnt_ref[...]
    if last:
        kept_weights_ref, kept_cnt_ref, sent_ref = outs
        half_width = width // 2
        keep = pl.ds(pl.multiple_of(core * half_width, half_width), half_width)
        send = pl.ds(pl.multiple_of((1 - core) * half_width, half_width), half_width)
        seen_buf[...] = jnp.broadcast_to(jnp.sum(seen, axis=1, keepdims=True), seen.shape)
        kept_cnt_ref[...] = seen_buf[keep, :]
        sent_ref[:, columns:] = seen_buf[send, :].astype(jnp.bfloat16)
        kept_weights_ref[...] = weights_buf[keep, :]
        targets = ((send, sent_ref),)
    else:
        outs[1][...] = seen
        targets = ((pl.ds(0, width), outs[0]),)
    chunk = min(columns, 512)
    for where, out in targets:
        for c in range(0, columns, chunk):
            part = slice(c, c + chunk)
            sums = lax.dot_general(
                weights_buf[where, :],
                rows_buf[:, part],
                (((1,), (0,)), ((), ())),
                preferred_element_type=jnp.float32,
            )
            if not first:
                sums += acc_ref[where, part]
            out[:, part] = sums.astype(out.dtype)


def keep_kernel(acc_ref, weights_ref, *refs):
    pieces, (kept_ref, rows_buf) = refs[:-2], refs[-2:]
    done = 0
    for piece in pieces:
        n = piece.shape[0]
        rows_buf[done : done + n, :] = piece[...]
        done += n
    rows, columns = kept_ref.shape
    core = lax.rem(lax.axis_index("img"), cores)
    keep = pl.ds(pl.multiple_of(core * rows, rows), rows)
    chunk = min(columns, 512)
    for c in range(0, columns, chunk):
        part = slice(c, c + chunk)
        kept_ref[:, part] = acc_ref[keep, part] + lax.dot_general(
            weights_ref[...],
            rows_buf[:, part],
            (((1,), (0,)), ((), ())),
            preferred_element_type=jnp.float32,
        )


def final_kernel(kept_ref, kept_cnt_ref, got_ref, proj_ref, out_ref):
    rows, columns = out_ref.shape
    core = lax.rem(lax.axis_index("img"), cores)
    here = pl.ds(pl.multiple_of(pl.program_id(0) * rows, rows), rows)
    first_row = (core * pl.num_programs(0) + pl.program_id(0)) * rows
    counts = kept_cnt_ref[here, 0:1] + got_ref[here, columns : columns + 1].astype(jnp.float32)
    sums = kept_ref[here, :] + got_ref[here, :columns].astype(jnp.float32)
    prior = prior_weight * proj_ref[pl.ds(pl.multiple_of(first_row, rows), rows), :].astype(
        jnp.float32
    )
    out_ref[...] = (sums + prior) * (1.0 / (counts + prior_weight))


def gathered_body(n_img, n_ori, images, precision, projections, tile_mask):
    n = n_img * n_ori
    shard, columns = images.shape
    orient = projections.shape[0]
    chips = n_img // cores
    width = orient // chips
    blocks, tiles = tile_mask.shape
    f32 = jnp.float32
    limit = pltpu.CompilerParams(vmem_limit_bytes=14 * 2**20)

    def swap(a, even, odd=None):
        masks = [d[0] * cores * n_ori + d[1] for d in (even, odd or even)]
        return lax.ppermute(a, both, [(i, i ^ masks[i // n_ori % cores]) for i in range(n)])

    def moved(shards, even, odd=None):
        odd = odd or even
        return tuple(
            ((e[0] ^ even[0], e[1] ^ even[1]), (o[0] ^ odd[0], o[1] ^ odd[1])) for e, o in shards
        )

    x, y = (0, 1), (1, 0)
    near, far = (x, y), (y, x)

    def sent(piece, even, odd=None):
        return moved(piece[0], even, odd), swap(piece[1], even, odd)

    def together(values):
        leaves, tree = jax.tree.flatten(values)
        arrays = iter(lax.optimization_barrier([a for a in leaves if not isinstance(a, int)]))
        return tree.unflatten([a if isinstance(a, int) else next(arrays) for a in leaves])

    lowered = images.astype(jnp.bfloat16)
    own = ((((0, 0), (0, 0)),), lowered)
    near_slab, far_slab = sent(own, (2, 0)), sent(own, (4, 0))
    own_a, own_b = sent(own, *near), sent(own, *far)

    prec_row = precision.reshape(1, -1)
    rows = prec_row.shape[1]
    held, held_chip, half_row, half_col = pl.pallas_call(
        functools.partial(load_kernel, chips),
        in_specs=[pl.BlockSpec(memory_space=pltpu.HBM)],
        out_specs=[vmem] * 4,
        out_shape=[
            pltpu.VMEM(projections.shape, projections.dtype),
            jax.ShapeDtypeStruct((width, columns), projections.dtype),
            jax.ShapeDtypeStruct((8, orient), f32),
            jax.ShapeDtypeStruct((width, lanes), f32),
        ],
        scratch_shapes=[pltpu.SemaphoreType.DMA((chips + 1,))],
        compiler_params=limit,
        cost_estimate=pl.CostEstimate(flops=0, bytes_accessed=0, transcendentals=0),
        name="load",
    )(pltpu.with_memory_space_constraint(projections, pltpu.HBM))
    held = pltpu.with_memory_space_constraint(held, pltpu.VMEM)
    own_a, own_b, held_chip, half_row, half_col = together(
        (own_a, own_b, held_chip, half_row, half_col)
    )
    own_c = sent(own_a, *far)
    whole = lambda i: (0, 0)
    scores, stats = pl.pallas_call(
        functools.partial(scores_kernel, chips),
        in_specs=[smem] + [vmem] * 6,
        out_specs=[vmem] * 2,
        out_shape=[
            pltpu.VMEM((rows, orient), f32),
            jax.ShapeDtypeStruct((8, rows), f32),
        ],
        scratch_shapes=[pltpu.VMEM((rows, columns), jnp.bfloat16)],
        compiler_params=limit,
        cost_estimate=pl.CostEstimate(flops=0, bytes_accessed=0, transcendentals=0),
        name="scores",
    )(tile_mask, prec_row, half_row, lowered, own_a[1], own_b[1], held)
    theirs = swap(stats, x)
    meta = pl.pallas_call(
        meta_kernel,
        in_specs=[smem, vmem, vmem, vmem],
        out_specs=vmem,
        out_shape=jax.ShapeDtypeStruct((n_ori, 8, shard), f32),
        compiler_params=limit,
        cost_estimate=pl.CostEstimate(flops=0, bytes_accessed=0, transcendentals=0),
        name="meta",
    )(tile_mask, prec_row, stats, theirs)
    from_y = swap(meta, y)
    far_slab, near_slab, own_c, meta, scores = together(
        (far_slab, near_slab, own_c, meta, scores)
    )
    last_slab = sent(far_slab, (2, 0))
    far_a, far_b = sent(far_slab, *near), sent(far_slab, *far)
    cut = 4
    posteriors = pl.pallas_call(
        posterior_kernel,
        grid=(cut,),
        in_specs=[
            vmem,
            pl.BlockSpec((8, rows), whole),
            pl.BlockSpec((8, rows), whole),
        ],
        out_specs=pl.BlockSpec((rows, orient // cut), lambda i: (0, i)),
        out_shape=jax.ShapeDtypeStruct((rows, orient), jnp.bfloat16),
        compiler_params=limit,
        cost_estimate=pl.CostEstimate(flops=0, bytes_accessed=0, transcendentals=0),
        name="posterior",
    )(scores, stats, theirs)

    far_a, far_b, last_slab, from_y, meta, posteriors = together(
        (far_a, far_b, last_slab, from_y, meta, posteriors)
    )
    far_c = sent(far_a, *far)
    last_a, last_b = sent(last_slab, *near), sent(last_slab, *far)
    metas = jnp.concatenate([meta, from_y], axis=0)
    metas = jnp.concatenate([metas, swap(metas, (2, 0))], axis=0)
    metas = [metas, swap(metas, (4, 0))]
    metas, own_b, own_c = together((metas, own_b, own_c))
    by_z = shard // 4 * 3
    near_b = moved(own_b[0], (2, 0)), swap(own_b[1][:by_z], (2, 0))
    near_c = sent(own_c, (2, 0))

    def add(group, state, last):
        shapes = tuple(shards for shards, _ in group)
        pieces = [a for _, a in group]
        images_here = sum(a.shape[0] for a in pieces)
        first = state is None
        if last:
            out_shape = [
                jax.ShapeDtypeStruct((width // 2, images_here), jnp.bfloat16),
                jax.ShapeDtypeStruct((width // 2, lanes), f32),
                jax.ShapeDtypeStruct((width // 2, columns + lanes), jnp.bfloat16),
            ]
        else:
            out_shape = [
                jax.ShapeDtypeStruct((width, columns), f32),
                jax.ShapeDtypeStruct((width, lanes), f32),
            ]
        n_ins = 2 + len(metas) + len(pieces) + (0 if first else 2)
        return pl.pallas_call(
            functools.partial(sums_kernel, len(metas), tiles * cores // n_img, shapes, first, last),
            in_specs=[vmem] * n_ins,
            out_specs=[vmem] * len(out_shape),
            out_shape=out_shape,
            input_output_aliases={} if first or last else {n_ins - 2: 0, n_ins - 1: 1},
            scratch_shapes=[
                pltpu.VMEM((images_here, columns), jnp.bfloat16),
                pltpu.VMEM((width, images_here), jnp.bfloat16),
                pltpu.VMEM((width, lanes), f32),
            ],
            compiler_params=limit,
        cost_estimate=pl.CostEstimate(flops=0, bytes_accessed=0, transcendentals=0),
            name="sums",
        )(half_col, held_chip, *metas, *pieces, *(state or ()))

    state = add([own, own_a, own_b, own_c], None, False)
    state = add([near_slab, far_slab, far_a, far_b], state, False)
    state, near_slab, far_c, last_a = together((state, near_slab, far_c, last_a))
    last_c = sent(last_a, *far)
    near_a = sent(near_slab, *near)
    near_b_low = (), swap(near_slab[1][by_z:], *far)
    state, last_b = together((state, last_b))
    state = add([far_c, last_slab, last_a, last_b], state, False)
    final_group = [near_a, near_b, near_b_low, near_c, last_c]
    kept_weights, kept_cnt, sent_away = add(final_group, state, True)
    got = lax.ppermute(sent_away, both, [(i, i ^ n_ori) for i in range(n)])
    last_pieces = [a for _, a in final_group]
    kept = pl.pallas_call(
        keep_kernel,
        in_specs=[vmem] * (2 + len(last_pieces)),
        out_specs=vmem,
        out_shape=jax.ShapeDtypeStruct((width // 2, columns), f32),
        scratch_shapes=[pltpu.VMEM((kept_weights.shape[1], columns), jnp.bfloat16)],
        compiler_params=limit,
        cost_estimate=pl.CostEstimate(flops=0, bytes_accessed=0, transcendentals=0),
        name="keep",
    )(state[0], kept_weights, *last_pieces)
    out_rows = width // 2
    cut = 2
    refined = pl.pallas_call(
        final_kernel,
        grid=(cut,),
        in_specs=[vmem] * 4,
        out_specs=pl.BlockSpec((out_rows // cut, columns), lambda i: (i, 0)),
        out_shape=jax.ShapeDtypeStruct((out_rows, columns), f32),
        compiler_params=limit,
        cost_estimate=pl.CostEstimate(flops=0, bytes_accessed=0, transcendentals=0),
        name="final",
    )(kept, kept_cnt, got, held_chip)
    return posteriors, refined


def solution(mesh):
    n_img, n_ori = mesh.shape["img"], mesh.shape["ori"]

    def body(images, precision, projections, tile_mask):
        shard, columns = images.shape
        orient = projections.shape[0]
        blocks, tiles = tile_mask.shape
        gathered_bytes = 2 * images.size * n_img * n_ori // cores
        fits = (
            n_ori == 2
            and n_img == 8 * cores
            and blocks == n_ori
            and shard % lanes == 0
            and tiles * cores % n_img == 0
            and orient % (tiles * lanes) == 0
            and tiles <= shard
            and gathered_bytes <= 16 * 2**20
        )
        if fits:
            return gathered_body(n_img, n_ori, images, precision, projections, tile_mask)
        return reduced_body(images, precision, projections, tile_mask)

    return jax.shard_map(
        body,
        mesh=mesh,
        in_specs=(P(("img", "ori"), None), P("img"), P("ori", None), P("img", "ori")),
        out_specs=(P("img", "ori"), P(("ori", "img"), None)),
        check_vma=False,
    )
```
